128 devices in a mesh: seq: 8 (over x, core), dp: 16 (over z, y).
Axes of the slice: x: 4, y: 4, z: 4, core: 2. Of those that a mesh axis runs over, the one named last changes fastest.
Arguments:
- text_rows: bfloat16 [2, 3072, 4096], P(None, 'seq', 'dp'), may hold values from -7 to 7
- latents: bfloat16 [16, 256, 32], P('dp', 'seq'), may hold values from -6 to 6
- image_seq: int32 [16], replicated, may hold values from 0 to 1, as said below
- image_start: int32 [16], replicated, may hold values from 0 to 2816, as said below
- norm_gain: float32 [4096], replicated, may hold values from 0.5 to 1.5
- w_patch: bfloat16 [32, 4096], replicated, may hold values from -1 to 1
- w_query: bfloat16 [4096, 4096], P(None, 'dp'), may hold values from -1 to 1
- w_key: bfloat16 [4096, 4096], P(None, 'dp'), may hold values from -1 to 1
- w_value: bfloat16 [4096, 4096], P(None, 'dp'), may hold values from -0.09375 to 0.09375
- out_grad: bfloat16 [2, 3072, 4096], P(None, 'seq', 'dp'), may hold values from -6 to 6
Outputs:
- attended: bfloat16 [2, 3072, 4096], P(None, 'seq', 'dp')
- latent_grad: float32 [16, 256, 32], P('dp', 'seq')
The draws below stay inside these ranges and needn't reach their ends.
Inputs may be any that keep to these rules, and one draw needn't show every extreme that they name: `image_seq`: each packed sequence holds exactly 8 images. `image_start`: the positions of a sequence fall into 8 aligned blocks of 384, each holding one whole image of that sequence.
All inputs are finite; a program needn't handle non-finite values.
Results may differ from the reference program's by a relative error of at most 0.028.
Values may be sent and summed in bfloat16 or wider, within the bound.
No kernel may reach another device: no remote copies, remote signals or barrier semaphores. Data moves between devices by JAX's collectives and lax.ppermute only.
A program may use at most 128 MiB of HBM per device.

```python
import jax
import jax.numpy as jnp
from jax import lax

D = 4096
HEADS = 32
HD = 128
PDIM = 32
PATCHES = 256
NSEQ = 2
LEN = 3072
IMAGES = 16
IMG_SEQ = 8


def place_images(key):
    slot_length = LEN // IMG_SEQ
    shuffled = jax.random.permutation(jax.random.fold_in(key, 21), IMAGES)
    jitter = jax.random.randint(jax.random.fold_in(key, 22), (IMAGES,), 0, slot_length - PATCHES + 1)
    extremes = jax.random.randint(jax.random.fold_in(key, 23), (2,), 0, NSEQ)
    jitter = jnp.where(shuffled == extremes[0], 0, jitter)
    jitter = jnp.where(shuffled == (IMG_SEQ - 1) * NSEQ + extremes[1], slot_length - PATCHES, jitter)
    owners = (shuffled % NSEQ).astype(jnp.int32)
    starts = (shuffled // NSEQ * slot_length + jitter).astype(jnp.int32)
    return (owners, starts)


def draw_image_seq(key, part):
    owners, starts = place_images(key)
    return owners


def draw_image_start(key, part):
    owners, starts = place_images(key)
    return starts


def draw_text_rows(key, part):
    key = jax.random.fold_in(key, 1)
    base = jax.random.truncated_normal(key, -6.0, 6.0, (NSEQ, LEN, D), jnp.float32)
    return base.astype(jnp.bfloat16)


def draw_w_query(key, part):
    key = jax.random.fold_in(key, 4)
    weight = jax.random.truncated_normal(key, -6.0, 6.0, (D, HEADS * HD), jnp.float32) * D ** (-0.5)
    return weight.astype(jnp.bfloat16)


def draw_w_key(key, part):
    key = jax.random.fold_in(key, 5)
    weight = jax.random.truncated_normal(key, -6.0, 6.0, (D, HEADS * HD), jnp.float32) * D ** (-0.5)
    return weight.astype(jnp.bfloat16)


def levels(key, dims, shards, smallest, top_value):
    def one(axis_at, parts):
        heights = jax.random.uniform(jax.random.fold_in(jax.random.fold_in(key, 6), axis_at), (parts,), jnp.float32, smallest / len(shards), top_value / len(shards))
        return jnp.repeat(jnp.exp(heights), dims[axis_at] // parts).reshape((-1,) + (1,) * (len(dims) - axis_at - 1))

    loudness = one(*shards[0])
    for cut in shards[1:]:
        loudness = loudness * one(*cut)
    return loudness


def bell_draw(rng, shape, spread, limit, pieces=(), held_as=jnp.bfloat16):
    level = levels(rng, shape, pieces, -0.22, 0.18) if pieces else 1.0
    values = jax.random.normal(rng, shape, jnp.float32) * spread * level
    return jnp.minimum(jnp.maximum(values, -limit), limit).astype(held_as)


def setup_inputs(seed: int = 0) -> dict:
    arg_keys = jax.random.split(jax.random.key(seed), 11)
    text_rows = draw_text_rows(jax.random.fold_in(arg_keys[10], 71), 0)
    latents = bell_draw(arg_keys[1], (IMAGES, PATCHES, PDIM), 1.0, 6.0, ((0, 16), (1, 8)))
    image_seq = draw_image_seq(jax.random.fold_in(arg_keys[10], 71), 0)
    image_start = draw_image_start(jax.random.fold_in(arg_keys[10], 71), 0)
    norm_gain = jnp.clip(1.0 + 0.1 * jax.random.normal(arg_keys[4], (D,), jnp.float32), 0.5, 1.5)
    w_patch = bell_draw(arg_keys[5], (PDIM, D), PDIM ** -0.5, 1.0)
    w_query = draw_w_query(jax.random.fold_in(arg_keys[10], 71), 0)
    w_key = draw_w_key(jax.random.fold_in(arg_keys[10], 71), 0)
    w_value = bell_draw(arg_keys[8], (D, HEADS * HD), D ** -0.5, 0.09375, ((1, 16),))
    out_grad = bell_draw(arg_keys[9], (NSEQ, LEN, HEADS * HD), 1.0, 6.0, ((1, 8), (2, 16)))
    return dict(text_rows=text_rows, latents=latents, image_seq=image_seq, image_start=image_start, norm_gain=norm_gain, w_patch=w_patch, w_query=w_query, w_key=w_key, w_value=w_value, out_grad=out_grad)


epsilon = 1e-05

def image_layout(image_seq, image_start, seq_count, places):
    owners = image_seq[None, :] == jnp.arange(seq_count, dtype=jnp.int32)[:, None]
    offset = places[:, None] - image_start[None, :]
    covers = owners[:, None, :] & (offset[None] >= 0) & (offset[None] < PATCHES)
    inside = jnp.any(covers, axis=2)
    labels = jnp.arange(image_seq.shape[0], dtype=jnp.int32)
    member = jnp.where(inside, lax.optimization_barrier(jnp.sum(jnp.where(covers, labels[None, None, :], 0), axis=2)), -1).astype(jnp.int32)
    patch_index = lax.optimization_barrier(jnp.sum(jnp.where(covers, labels[None, None, :] * PATCHES + offset[None], 0), axis=2)).astype(jnp.int32)
    return (inside, member, patch_index)

def one_head(queries, key_rows, value_rows, grad_rows, allowed):
    score_scale = HD ** (-0.5)
    scores = jnp.dot(queries, key_rows.T, preferred_element_type=jnp.float32) * score_scale
    masked = jnp.where(allowed, scores, -jnp.inf)
    row_max = lax.optimization_barrier(jnp.max(masked, axis=-1, keepdims=True))
    lifted = jnp.exp(masked - row_max)
    row_total = lax.optimization_barrier(jnp.sum(lifted, axis=-1, keepdims=True))
    attn_probs = lifted / row_total
    probs_b = attn_probs.astype(jnp.bfloat16)
    out_f = jnp.dot(probs_b, value_rows, preferred_element_type=jnp.float32)
    row_delta = lax.optimization_barrier(jnp.sum(grad_rows.astype(jnp.float32) * out_f, axis=-1, keepdims=True))
    d_probs = jnp.dot(grad_rows, value_rows.T, preferred_element_type=jnp.float32)
    d_scores = (attn_probs * (d_probs - row_delta) * score_scale).astype(jnp.bfloat16)
    d_query = jnp.dot(d_scores, key_rows, preferred_element_type=jnp.float32).astype(jnp.bfloat16)
    d_key = jnp.dot(d_scores.T, queries, preferred_element_type=jnp.float32).astype(jnp.bfloat16)
    d_value = jnp.dot(probs_b.T, grad_rows, preferred_element_type=jnp.float32).astype(jnp.bfloat16)
    return (out_f.astype(jnp.bfloat16), d_query, d_key, d_value)

def one_sequence(text_seq, patch_rows, inside, member, grad_seq, norm_gain, w_patch, w_query, w_key, w_value):
    length = text_seq.shape[0]
    places = jnp.arange(length, dtype=jnp.int32)
    allowed = (places[None, :] <= places[:, None]) | (member[:, None] == member[None, :]) & inside[:, None]
    embedded = jnp.dot(patch_rows, w_patch, preferred_element_type=jnp.float32).astype(jnp.bfloat16)
    hidden = jnp.where(inside[:, None], embedded, text_seq)
    hidden_f = hidden.astype(jnp.float32)
    inv_rms = lax.rsqrt(lax.optimization_barrier(jnp.mean(hidden_f * hidden_f, axis=-1, keepdims=True)) + epsilon)
    unit_rows = hidden_f * inv_rms
    normed = (unit_rows * norm_gain).astype(jnp.bfloat16)
    head_count = w_query.shape[1] // HD

    def heads_first(matrix):
        return matrix.reshape(length, head_count, HD).transpose(1, 0, 2)

    def heads_last(stacked):
        return stacked.transpose(1, 0, 2).reshape(length, head_count * HD)
    queries = heads_first(jnp.dot(normed, w_query, preferred_element_type=jnp.float32).astype(jnp.bfloat16))
    key_rows = heads_first(jnp.dot(normed, w_key, preferred_element_type=jnp.float32).astype(jnp.bfloat16))
    value_rows = heads_first(jnp.dot(normed, w_value, preferred_element_type=jnp.float32).astype(jnp.bfloat16))
    grad_rows = heads_first(grad_seq)

    def per_head(inputs):
        return one_head(inputs[0], inputs[1], inputs[2], inputs[3], allowed)
    out_heads, d_query, d_key, d_value = lax.map(per_head, (queries, key_rows, value_rows, grad_rows))
    attended = heads_last(out_heads)
    d_normed = jnp.dot(heads_last(d_query), w_query.T, preferred_element_type=jnp.float32)
    d_normed = d_normed + jnp.dot(heads_last(d_key), w_key.T, preferred_element_type=jnp.float32)
    d_normed = d_normed + jnp.dot(heads_last(d_value), w_value.T, preferred_element_type=jnp.float32)
    gained = norm_gain * d_normed
    d_hidden = inv_rms * (gained - unit_rows * lax.optimization_barrier(jnp.mean(unit_rows * gained, axis=-1, keepdims=True)))
    d_rows = jnp.dot(d_hidden, w_patch.astype(jnp.float32).T, precision=lax.Precision.HIGHEST)
    return (attended, d_rows)

def reference(text_rows, latents, image_seq, image_start, norm_gain, w_patch, w_query, w_key, w_value, out_grad):
    seq_count = text_rows.shape[0]
    length = text_rows.shape[1]
    inside, member, patch_index = image_layout(image_seq, image_start, seq_count, jnp.arange(length, dtype=jnp.int32))
    flat_patches = latents.reshape(IMAGES * PATCHES, PDIM)
    picked = jnp.take(flat_patches, patch_index, axis=0)

    def per_sequence(inputs):
        text_seq, patch_rows, inside_seq, member_seq, grad_seq = inputs
        return one_sequence(text_seq, patch_rows, inside_seq, member_seq, grad_seq, norm_gain, w_patch, w_query, w_key, w_value)
    attended, d_rows = lax.map(per_sequence, (text_rows, picked, inside, member, out_grad))

    def fetch_block(seq_index, start_index):
        zero_index = jnp.zeros((), jnp.int32)
        window = lax.dynamic_slice(d_rows, (seq_index.astype(jnp.int32), start_index.astype(jnp.int32), zero_index), (1, PATCHES, PDIM))
        return window[0]
    latent_grad = jax.vmap(fetch_block)(image_seq, image_start)
    return (attended, latent_grad)
```

```python
import math

import jax
import jax.numpy as jnp
from jax import lax
from jax.experimental import pallas as pl
from jax.experimental.pallas import tpu as pltpu
from jax.sharding import PartitionSpec as P

HD = 128
PATCHES = 256
PDIM = 32
BLOCK = 384
TEXT = BLOCK - PATCHES
IMAGES = 16
NSEQ = 2
D = 4096
epsilon = 1e-05
SCALE = HD ** (-0.5)
LN2 = math.log(2.0)
BF = jnp.bfloat16
F32 = jnp.float32
SEND_ROWS = NSEQ * TEXT + 16
KV_ROWS = NSEQ * TEXT + 32


def dot_nn(a, b):
    return lax.dot_general(a, b, (((1,), (0,)), ((), ())), preferred_element_type=F32)


def dot_nt(a, b):
    return lax.dot_general(a, b, (((1,), (1,)), ((), ())), preferred_element_type=F32)


def lane_place(a):
    rows = lax.broadcasted_iota(jnp.int32, (PDIM, 128), 0)
    lanes = lax.broadcasted_iota(jnp.int32, (PDIM, 128), 1)
    return jnp.where(lanes == rows + PDIM * a, 1.0, 0.0).astype(BF)


def own_offsets(seq_ref, start_ref, seat):
    offs = [jnp.int32(0), jnp.int32(0)]
    for i in range(IMAGES):
        rel = start_ref[i] - seat * BLOCK
        mine = (rel >= 0) & (rel < BLOCK)
        for g in range(NSEQ):
            offs[g] = jnp.where(mine & (seq_ref[i] == g), rel, offs[g])
    return offs


def pack_kernel(seq_ref, start_ref, seat_ref, text_ref, lat_ref, wp_ref, send_ref, inv_ref, u_ref):
    offs = own_offsets(seq_ref, start_ref, seat_ref[0])
    lat = lat_ref[...]
    wp = wp_ref[...]
    embedded = dot_nn(lat, wp).astype(BF)
    emb_f = embedded.astype(F32)
    inv = lax.rsqrt(jnp.sum(emb_f * emb_f, axis=1, keepdims=True) * (1.0 / D) + epsilon)
    inv_ref[...] = jnp.broadcast_to(inv, inv_ref.shape)
    u_ref[...] = dot_nt(embedded, wp)
    scaled = (lat.astype(F32) * inv).astype(BF)
    rows8 = lax.broadcasted_iota(jnp.int32, (8, PDIM), 0)
    cols8 = lax.broadcasted_iota(jnp.int32, (8, PDIM), 1)
    packed = jnp.zeros((8, 128), F32)
    for a in range(4):
        pick = jnp.where(cols8 == rows8 + 8 * a, 1.0, 0.0).astype(BF)
        part = dot_nn(pick, scaled).astype(BF)
        packed = packed + dot_nn(part, lane_place(a))
    tail = jnp.concatenate([packed, jnp.zeros((8, 128), F32)], axis=0)
    tail = jnp.concatenate([tail, jnp.zeros((16, 128), F32)], axis=1).astype(BF)
    row = lax.broadcasted_iota(jnp.int32, (TEXT, 256), 0)
    texts = []
    for g in range(NSEQ):
        low = text_ref[g, 0:TEXT, :].astype(F32)
        high = text_ref[g, PATCHES:BLOCK, :].astype(F32)
        texts.append(jnp.where(row < offs[g], low, high).astype(BF))
    for d in range(send_ref.shape[0]):
        for g in range(NSEQ):
            send_ref[d, g * TEXT : (g + 1) * TEXT, :] = texts[g]
        send_ref[d, NSEQ * TEXT :, :] = tail


FEATURE_STEP = 2


def project_kernel(x_ref, wq_ref, wk_ref, wv_ref, wp_ref, gain_ref, qt_ref, kv_ref, mt_ref, acc, ssq):
    step = pl.program_id(0)
    rows = NSEQ * TEXT
    lhs = []
    total = jnp.zeros((rows, 128), F32)
    for j in range(FEATURE_STEP):
        gain = gain_ref[:, 256 * j : 256 * (j + 1)]
        x = x_ref[j, 0:rows, :].astype(F32)
        squares = x * x
        total = total + squares[:, :128] + squares[:, 128:]
        text = (x * gain).astype(BF)
        patch = (wp_ref[:, 256 * j : 256 * (j + 1)].astype(F32) * gain).astype(BF)
        lhs.append(jnp.concatenate([text, patch], axis=0))
    left = jnp.concatenate(lhs, axis=1)

    @pl.when(step == 0)
    def _():
        acc[...] = jnp.zeros_like(acc)
        ssq[...] = jnp.zeros_like(ssq)

    ssq[...] += total
    for n, w_ref in enumerate((wq_ref, wk_ref, wv_ref)):
        acc[:, 256 * n : 256 * (n + 1)] += dot_nn(left, w_ref[...])

    @pl.when(step == pl.num_programs(0) - 1)
    def _():
        inv = lax.rsqrt(jnp.sum(ssq[...], axis=1, keepdims=True) * (1.0 / D) + epsilon)
        qt_ref[...] = (acc[0:rows, 0:256] * (inv * (SCALE / LN2))).astype(BF)
        kv_ref[0:rows, :] = (acc[0:rows, 256:768] * inv).astype(BF)
        mt_ref[...] = acc[rows:, :].astype(BF)


def lat_tiles(recv):
    tiles = recv[:, NSEQ * TEXT : NSEQ * TEXT + 8, 0:128]
    tiles = tiles.reshape(4, 4, 8, 128).transpose(0, 2, 1, 3)
    return tiles.reshape(32, 512)


def fold_max(s):
    return jnp.maximum(jnp.maximum(s[:, 0:128], s[:, 128:256]), s[:, 256:384])


def fold_sum(s):
    return s[:, 0:128] + s[:, 128:256] + s[:, 256:384]


def position(index, offset):
    patch = 32 * ((index & 63) >> 3) + 8 * (index >> 6) + (index & 7)
    t = index - PATCHES
    return jnp.where(
        index < PATCHES, offset + patch, jnp.where(t < offset, t, t + PATCHES)
    )


def attend_kernel(
    seq_ref, start_ref, seat_ref, cg_ref, qt_ref, mt_ref, grad_ref,
    out_ref, z_ref,
    labels, tiles, wide, keys, values, scores, probs, q_s, g_s, o_s, m_s, l_s, zt, zq,
):
    seat = seat_ref[0]
    offs = own_offsets(seq_ref, start_ref, seat)
    for i in range(IMAGES):
        labels[seq_ref[i] * 8 + lax.div(start_ref[i], BLOCK)] = i

    wide[...] = jnp.zeros_like(wide)
    for a in range(4):
        wide[128 * a + PDIM * a : 128 * a + PDIM * (a + 1), :] = mt_ref[...]
    for j in range(8):
        part = cg_ref[j, NSEQ * TEXT :, :].astype(F32)
        for i in range(IMAGES):
            tiles[i, 8 * j : 8 * (j + 1), :] = part[
                8 * (i // 4) : 8 * (i // 4 + 1), 128 * (i % 4) : 128 * (i % 4 + 1)
            ]
    zt[...] = jnp.zeros_like(zt)

    rows = lax.broadcasted_iota(jnp.int32, (BLOCK, BLOCK), 0)
    cols = lax.broadcasted_iota(jnp.int32, (BLOCK, BLOCK), 1)

    def heads(h):
        return slice(h * HD, (h + 1) * HD)

    for g in range(NSEQ):
        off = offs[g]
        own = labels[g * 8 + seat]
        own_tile = tiles[own].astype(BF)
        for a in range(4):
            q_s[64 * a : 64 * (a + 1), :] = (
                dot_nn(own_tile, wide[128 * a : 128 * (a + 1), 0:256]) * (SCALE / LN2)
            ).astype(BF)
        q_s[PATCHES:, :] = qt_ref[g * TEXT : (g + 1) * TEXT, :]
        place = jnp.where(cols == position(rows, off), 1.0, 0.0).astype(BF)
        g_s[...] = dot_nn(place, grad_ref[g]).astype(BF)

        def score_block(b, diagonal):
            label = labels[g * 8 + b]
            tile = tiles[label].astype(BF)
            for a in range(4):
                kv = dot_nn(tile, wide[128 * a : 128 * (a + 1), 256:768]).astype(BF)
                keys[b, 64 * a : 64 * (a + 1), :] = kv[:, 0:256]
                values[b, 64 * a : 64 * (a + 1), :] = kv[:, 256:512]
            keys[b, PATCHES:, :] = cg_ref[b, g * TEXT : (g + 1) * TEXT, 0:256]
            values[b, PATCHES:, :] = cg_ref[b, g * TEXT : (g + 1) * TEXT, 256:512]
            for h in range(2):
                s = dot_nt(q_s[:, heads(h)], keys[b, :, heads(h)])
                if diagonal:
                    reach = jnp.where(rows < PATCHES, off + (PATCHES - 1), position(rows, off))
                    s = jnp.where(position(cols, off) <= reach, s, -jnp.inf)
                    m_s[h] = fold_max(s)
                else:
                    m_s[h] = jnp.maximum(m_s[h], fold_max(s))
                scores[h, b] = s

        score_block(seat, True)

        def score_body(b, carry):
            score_block(b, False)
            return carry

        lax.fori_loop(0, seat, score_body, 0)

        o_s[...] = jnp.zeros_like(o_s)
        l_s[...] = jnp.zeros_like(l_s)
        tops = [jnp.max(m_s[h], axis=1, keepdims=True) for h in range(2)]
        for h in range(2):
            m_s[h] = jnp.broadcast_to(tops[h], (BLOCK, 128))

        def prob_body(b, carry):
            for h in range(2):
                top = m_s[h]
                p = jnp.exp2(scores[h, b] - jnp.concatenate([top, top, top], axis=1))
                l_s[h] += fold_sum(p)
                p = p.astype(BF)
                probs[h, b] = p
                o_s[h] += dot_nn(p, values[b, :, heads(h)])
            return carry

        lax.fori_loop(0, seat + 1, prob_body, 0)

        outs = []
        xk = []
        xv = []
        for h in range(2):
            inv = 1.0 / jnp.sum(l_s[h], axis=1, keepdims=True)
            out = o_s[h] * inv
            outs.append(out.astype(BF))
            scaled = (g_s[:, heads(h)].astype(F32) * inv).astype(BF)
            delta = jnp.sum(scaled.astype(F32) * out, axis=1, keepdims=True)
            m_s[h] = jnp.broadcast_to(delta, (BLOCK, 128))
            g_s[:, heads(h)] = scaled
            mk = mt_ref[:, 256 + h * HD : 256 + (h + 1) * HD]
            mv = mt_ref[:, 512 + h * HD : 512 + (h + 1) * HD]
            xk.append((dot_nt(mk, q_s[:, heads(h)]) * LN2).astype(BF))
            xv.append(dot_nt(mv, scaled).astype(BF))
        out_c = jnp.concatenate(outs, axis=1)
        back = jnp.where(rows == position(cols, off), 1.0, 0.0).astype(BF)
        out_ref[g] = dot_nn(back, out_c).astype(BF)
        zq[...] = jnp.zeros_like(zq)

        def grad_body(b, carry):
            label = labels[g * 8 + b]
            total = zt[label]
            for h in range(2):
                delta = m_s[h]
                wide_delta = jnp.concatenate([delta, delta, delta], axis=1)
                value = values[b, :, heads(h)]
                dp = dot_nt(g_s[0:PATCHES, heads(h)], value)
                ds = (probs[h, b, 0:PATCHES, :].astype(F32) * (dp - wide_delta[0:PATCHES])).astype(BF)
                dp_text = dot_nt(g_s[PATCHES:, heads(h)], value[0:PATCHES])
                ds_text = (
                    probs[h, b, PATCHES:, 0:PATCHES].astype(F32)
                    * (dp_text - wide_delta[PATCHES:, 0:PATCHES])
                ).astype(BF)
                mq = mt_ref[:, heads(h)]
                km = (dot_nt(keys[b, :, heads(h)], mq) * SCALE).astype(BF)
                zq[...] += dot_nn(ds, km)
                total = total + dot_nn(xk[h][:, 0:PATCHES], ds[:, 0:PATCHES])
                total = total + dot_nn(xk[h][:, PATCHES:], ds_text)
                total = total + dot_nn(xv[h], probs[h, b, :, 0:PATCHES])
            zt[label] = total
            return carry

        lax.fori_loop(0, seat + 1, grad_body, 0)
        zt[own] += zq[...].T

    for i in range(IMAGES):
        flat = zt[i].T.astype(BF)
        dense = jnp.zeros((64, 128), F32)
        for a in range(4):
            dense = dense + dot_nn(flat[64 * a : 64 * (a + 1)], lane_place(a))
        z_ref[i] = dense.astype(BF)


def finish_kernel(recv_ref, lat_ref, inv_ref, u_ref, out_ref):
    total = jnp.sum(recv_ref[...].astype(F32), axis=0)
    for a in range(4):
        at = slice(8 * a, 8 * (a + 1))
        z = total[:, PDIM * a : PDIM * (a + 1)]
        inv = inv_ref[at, :][:, 0:1]
        inner = jnp.sum(lat_ref[at, :] * z, axis=1, keepdims=True)
        out_ref[at, :] = inv * (z - u_ref[at, :] * (inv * inv * inner * (1.0 / D)))


def gather_by_exchange(block, axis, copies):
    return lax.all_to_all(jnp.broadcast_to(block[None], (copies,) + block.shape), axis, 0, 0)


def on_device(
    text_rows, latents, image_seq, image_start, norm_gain, w_patch, w_query, w_key, w_value, out_grad
):
    seats = lax.axis_size("seq")
    groups = lax.axis_size("dp")
    seat = lax.axis_index("seq").astype(jnp.int32).reshape(1)
    lat = latents.reshape(PDIM, PDIM)
    smem = pl.BlockSpec(memory_space=pltpu.SMEM)
    vmem = pl.BlockSpec(memory_space=pltpu.VMEM)
    send, inv, u = pl.pallas_call(
        pack_kernel,
        out_shape=(
            jax.ShapeDtypeStruct((groups, SEND_ROWS, 256), BF),
            jax.ShapeDtypeStruct((PDIM, 128), F32),
            jax.ShapeDtypeStruct((PDIM, PDIM), F32),
        ),
        in_specs=[smem] * 3 + [vmem] * 3,
        out_specs=(vmem,) * 3,
        compiler_params=pltpu.CompilerParams(vmem_limit_bytes=32 * 2**20),
        name="pack",
    )(image_seq, image_start, seat, text_rows, lat, w_patch)
    recv = lax.all_to_all(send, "dp", 0, 0)

    steps = groups // FEATURE_STEP
    width = 256 * FEATURE_STEP
    weight_spec = pl.BlockSpec((width, 256), lambda d: (d, 0))
    qt, kv, mt = pl.pallas_call(
        project_kernel,
        grid=(steps,),
        out_shape=(
            jax.ShapeDtypeStruct((NSEQ * TEXT, 256), BF),
            jax.ShapeDtypeStruct((NSEQ * TEXT, 512), BF),
            jax.ShapeDtypeStruct((PDIM, 768), BF),
        ),
        in_specs=[
            pl.BlockSpec((FEATURE_STEP, SEND_ROWS, 256), lambda d: (d, 0, 0)),
            weight_spec,
            weight_spec,
            weight_spec,
            pl.BlockSpec((PDIM, width), lambda d: (0, d)),
            pl.BlockSpec((1, width), lambda d: (0, d)),
        ],
        out_specs=(
            pl.BlockSpec((NSEQ * TEXT, 256), lambda d: (0, 0)),
            pl.BlockSpec((NSEQ * TEXT, 512), lambda d: (0, 0)),
            pl.BlockSpec((PDIM, 768), lambda d: (0, 0)),
        ),
        scratch_shapes=[
            pltpu.VMEM((NSEQ * TEXT + PDIM, 768), F32),
            pltpu.VMEM((NSEQ * TEXT, 128), F32),
        ],
        compiler_params=pltpu.CompilerParams(vmem_limit_bytes=32 * 2**20),
        name="project",
    )(recv, w_query, w_key, w_value, w_patch, norm_gain.reshape(1, D))
    gathered = gather_by_exchange(jnp.concatenate([kv, lat_tiles(recv)], axis=0), "seq", seats)

    attended, z = pl.pallas_call(
        attend_kernel,
        out_shape=(
            jax.ShapeDtypeStruct((NSEQ, BLOCK, 256), BF),
            jax.ShapeDtypeStruct((IMAGES, 64, 128), BF),
        ),
        in_specs=[smem] * 3 + [vmem] * 4,
        out_specs=(vmem,) * 2,
        scratch_shapes=[
            pltpu.SMEM((IMAGES,), jnp.int32),
            pltpu.VMEM((IMAGES, 64, 128), F32),
            pltpu.VMEM((512, 768), BF),
            pltpu.VMEM((8, BLOCK, 256), BF),
            pltpu.VMEM((8, BLOCK, 256), BF),
            pltpu.VMEM((2, 8, BLOCK, BLOCK), F32),
            pltpu.VMEM((2, 8, BLOCK, BLOCK), BF),
            pltpu.VMEM((BLOCK, 256), BF),
            pltpu.VMEM((BLOCK, 256), BF),
            pltpu.VMEM((2, BLOCK, HD), F32),
            pltpu.VMEM((2, BLOCK, 128), F32),
            pltpu.VMEM((2, BLOCK, 128), F32),
            pltpu.VMEM((IMAGES, PDIM, PATCHES), F32),
            pltpu.VMEM((PATCHES, PDIM), F32),
        ],
        compiler_params=pltpu.CompilerParams(vmem_limit_bytes=48 * 2**20),
        name="attend",
    )(image_seq, image_start, seat, gathered, qt, mt, out_grad)

    parts = lax.all_to_all(z.reshape(groups * seats, 8, 128), ("dp", "seq"), 0, 0)
    grad = pl.pallas_call(
        finish_kernel,
        out_shape=jax.ShapeDtypeStruct((PDIM, PDIM), F32),
        in_specs=[vmem] * 4,
        out_specs=vmem,
        compiler_params=pltpu.CompilerParams(vmem_limit_bytes=32 * 2**20),
        name="finish",
    )(parts, lat.astype(F32), inv, u)
    return (attended, grad.reshape(latents.shape))


def solution(mesh):
    in_specs = (
        P(None, "seq", "dp"),
        P("dp", "seq", None),
        P(),
        P(),
        P(),
        P(),
        P(None, "dp"),
        P(None, "dp"),
        P(None, "dp"),
        P(None, "seq", "dp"),
    )
    out_specs = (P(None, "seq", "dp"), P("dp", "seq", None))
    return jax.shard_map(
        on_device, mesh=mesh, in_specs=in_specs, out_specs=out_specs, check_vma=False
    )
```

```python
import functools
import math

import jax
import jax.numpy as jnp
from jax import lax
from jax.experimental import pallas as pl
from jax.experimental.pallas import tpu as pltpu
from jax.sharding import PartitionSpec as P

HD = 128
PATCHES = 256
PDIM = 32
BLOCK = 384
TEXT = BLOCK - PATCHES
IMAGES = 16
NSEQ = 2
D = 4096
epsilon = 1e-05
SCALE = HD ** (-0.5)
LN2 = math.log(2.0)
BF = jnp.bfloat16
F32 = jnp.float32
SEND_ROWS = NSEQ * TEXT + 16
KV_ROWS = NSEQ * TEXT + 32


def dot_nn(a, b):
    return lax.dot_general(a, b, (((1,), (0,)), ((), ())), preferred_element_type=F32)


def dot_nt(a, b):
    return lax.dot_general(a, b, (((1,), (1,)), ((), ())), preferred_element_type=F32)


def own_offsets(seq_ref, start_ref, seat):
    offs = [jnp.int32(0), jnp.int32(0)]
    for i in range(IMAGES):
        rel = start_ref[i] - seat * BLOCK
        mine = (rel >= 0) & (rel < BLOCK)
        for g in range(NSEQ):
            offs[g] = jnp.where(mine & (seq_ref[i] == g), rel, offs[g])
    return offs


def pack_kernel(
    seq_hbm, start_hbm, seat_ref, text_hbm, lat_hbm, wp_hbm,
    send_ref, inv_ref, u_ref,
    seq_ref, start_ref, text_ref, lat_ref, wp_ref, sems,
):
    pairs = (
        (seq_hbm, seq_ref), (start_hbm, start_ref), (lat_hbm, lat_ref), (wp_hbm, wp_ref),
        (text_hbm, text_ref),
    )
    copies = [pltpu.make_async_copy(a, b, sems.at[n]) for n, (a, b) in enumerate(pairs)]
    for copy in copies:
        copy.start()
    copies[2].wait()
    copies[3].wait()
    lat = lat_ref[...]
    wp = wp_ref[...]
    embedded = dot_nn(lat, wp).astype(BF)
    emb_f = embedded.astype(F32)
    inv = lax.rsqrt(jnp.sum(emb_f * emb_f, axis=1, keepdims=True) * (1.0 / D) + epsilon)
    inv_ref[...] = jnp.broadcast_to(inv, inv_ref.shape)
    u_ref[...] = dot_nt(embedded, wp)
    scaled = lat.astype(F32) * inv
    packed = jnp.concatenate([scaled[8 * a : 8 * (a + 1)] for a in range(4)], axis=1)
    tail = jnp.concatenate([packed, jnp.zeros((8, 128), F32)], axis=0)
    tail = jnp.concatenate([tail, jnp.zeros((16, 128), F32)], axis=1).astype(BF)
    copies[0].wait()
    copies[1].wait()
    offs = own_offsets(seq_ref, start_ref, seat_ref[0])
    copies[4].wait()
    row = lax.broadcasted_iota(jnp.int32, (TEXT, 256), 0)
    texts = []
    for g in range(NSEQ):
        low = text_ref[g, 0:TEXT, :].astype(F32)
        high = text_ref[g, PATCHES:BLOCK, :].astype(F32)
        texts.append(jnp.where(row < offs[g], low, high).astype(BF))
    for d in range(send_ref.shape[0]):
        for g in range(NSEQ):
            send_ref[d, g * TEXT : (g + 1) * TEXT, :] = texts[g]
        send_ref[d, NSEQ * TEXT :, :] = tail


def project_kernel(
    x_ref, wq_ref, wk_ref, wv_hbm, wp_ref, gain_ref, qt_ref, block_ref, mt_ref, left, wv_ref, sem
):
    copy = pltpu.make_async_copy(wv_hbm, wv_ref, sem)
    copy.start()
    rows = NSEQ * TEXT
    ssq = jnp.zeros((rows, 128), F32)
    tiles = []
    for d in range(x_ref.shape[0]):
        at = slice(256 * d, 256 * (d + 1))
        gain = gain_ref[:, at]
        x = x_ref[d, 0:rows, :].astype(F32)
        squares = x * x
        ssq = ssq + squares[:, :128] + squares[:, 128:]
        left[0:rows, at] = (x * gain).astype(BF)
        left[rows:, at] = (wp_ref[:, at].astype(F32) * gain).astype(BF)
        tiles.append(x_ref[d, rows : rows + 16, 0:128].astype(F32)[0:8])
    inv = lax.rsqrt(jnp.sum(ssq, axis=1, keepdims=True) * (1.0 / D) + epsilon)
    lat = [jnp.concatenate(tiles[4 * n : 4 * (n + 1)], axis=1) for n in range(4)]
    block_ref[rows:, :] = jnp.concatenate(lat, axis=0).astype(BF)
    query = dot_nn(left[...], wq_ref[...])
    qt_ref[...] = (query[0:rows] * (inv * (SCALE / LN2))).astype(BF)
    mt_ref[:, 0:256] = query[rows:].astype(BF)
    key = dot_nn(left[...], wk_ref[...])
    block_ref[0:rows, 0:256] = (key[0:rows] * inv).astype(BF)
    mt_ref[:, 256:512] = key[rows:].astype(BF)
    copy.wait()
    value = dot_nn(left[...], wv_ref[...])
    block_ref[0:rows, 256:512] = (value[0:rows] * inv).astype(BF)
    mt_ref[:, 512:768] = value[rows:].astype(BF)


def fold_max(s):
    return functools.reduce(jnp.maximum, [s[:, 128 * n : 128 * (n + 1)] for n in range(6)])


def fold_sum(s):
    return functools.reduce(jnp.add, [s[:, 128 * n : 128 * (n + 1)] for n in range(6)])


def position(index, offset):
    patch = 32 * ((index & 63) >> 3) + 8 * (index >> 6) + (index & 7)
    t = index - PATCHES
    return jnp.where(
        index < PATCHES, offset + patch, jnp.where(t < offset, t, t + PATCHES)
    )


def heads(h):
    return slice(h * HD, (h + 1) * HD)


CHAINS = [(g, h) for g in range(NSEQ) for h in range(2)]


def attend_kernel(
    seq_ref, start_ref, seat_ref, same_ref, other_ref, qt_ref, mt_ref, grad_ref,
    out_ref, z_ref,
    labels, tiles, wide, keys, values, scores, probs, q_s, g_s, o_s, m_s, l_s, zt, zq,
):
    seat = seat_ref[0]
    chip, core = seat >> 1, seat & 1
    offs = own_offsets(seq_ref, start_ref, seat)
    for i in range(IMAGES):
        labels[seq_ref[i] * 8 + lax.div(start_ref[i], BLOCK)] = i

    wide[...] = jnp.zeros_like(wide)
    for a in range(4):
        wide[128 * a + PDIM * a : 128 * a + PDIM * (a + 1), :] = mt_ref[...]
    for k in range(4):
        pair = (chip - k) & 3
        for ref, parity in ((same_ref, core), (other_ref, 1 - core)):
            part = ref[k, NSEQ * TEXT :, :].astype(F32)
            at = pl.multiple_of((2 * pair + parity) * 8, 8)
            for i in range(IMAGES):
                tiles[i, pl.ds(at, 8), :] = part[
                    8 * (i // 4) : 8 * (i // 4 + 1), 128 * (i % 4) : 128 * (i % 4 + 1)
                ]
            at = pl.ds(pl.multiple_of(2 * PATCHES + TEXT * parity, TEXT), TEXT)
            for g in range(NSEQ):
                keys[g, pair, at, :] = ref[k, g * TEXT : (g + 1) * TEXT, 0:256]
                values[g, pair, at, :] = ref[k, g * TEXT : (g + 1) * TEXT, 256:512]

    rows = lax.broadcasted_iota(jnp.int32, (BLOCK, BLOCK), 0)
    cols = lax.broadcasted_iota(jnp.int32, (BLOCK, BLOCK), 1)
    for g in range(NSEQ):
        own_tile = tiles[labels[g * 8 + seat]].astype(BF)
        in_order = jnp.concatenate([tiles[labels[g * 8 + b]] for b in range(8)], axis=0).astype(BF)
        for a in range(4):
            patch = wide[128 * a : 128 * (a + 1), :]
            q_s[g, 64 * a : 64 * (a + 1), :] = (
                dot_nn(own_tile, patch[:, 0:256]) * (SCALE / LN2)
            ).astype(BF)
            kv = dot_nn(in_order, patch[:, 256:768]).astype(BF)
            for b in range(8):
                at = slice(PATCHES * (b % 2) + 64 * a, PATCHES * (b % 2) + 64 * (a + 1))
                keys[g, b // 2, at, :] = kv[64 * b : 64 * (b + 1), 0:256]
                values[g, b // 2, at, :] = kv[64 * b : 64 * (b + 1), 256:512]
        q_s[g, PATCHES:, :] = qt_ref[g * TEXT : (g + 1) * TEXT, :]
        place = jnp.where(cols == position(rows, offs[g]), 1.0, 0.0).astype(BF)
        g_s[g] = dot_nn(place, grad_ref[g]).astype(BF)

    def each(count, body):
        def step(p, carry):
            body(p)
            return carry

        lax.fori_loop(0, count, step, 0)

    q_row = lax.broadcasted_iota(jnp.int32, (BLOCK, 2 * BLOCK), 0)
    k_col = lax.broadcasted_iota(jnp.int32, (BLOCK, 2 * BLOCK), 1)
    in_image = k_col < 2 * PATCHES
    second = jnp.where(in_image, k_col >> 8, (k_col - 2 * PATCHES) >> 7)
    k_row = jnp.where(in_image, k_col & (PATCHES - 1), PATCHES + (k_col & (TEXT - 1)))

    def score(p, diagonal=False):
        for n, (g, h) in enumerate(CHAINS):
            s = dot_nt(q_s[g, :, heads(h)], keys[g, p, :, heads(h)])
            if diagonal:
                off = offs[g]
                reach = jnp.where(q_row < PATCHES, off + (PATCHES - 1), position(q_row, off))
                place = position(k_row, off) + BLOCK * (second - core)
                s = jnp.where(place <= reach, s, -jnp.inf)
                m_s[n] = fold_max(s)
            else:
                m_s[n] = jnp.maximum(m_s[n], fold_max(s))
            scores[n, p] = s

    score(chip, True)
    each(chip, score)

    o_s[...] = jnp.zeros_like(o_s)
    l_s[...] = jnp.zeros_like(l_s)
    for n in range(4):
        m_s[n] = jnp.broadcast_to(jnp.max(m_s[n], axis=1, keepdims=True), (BLOCK, 128))

    def weigh(p):
        for n, (g, h) in enumerate(CHAINS):
            top = m_s[n]
            lifted = jnp.exp2(scores[n, p] - jnp.concatenate([top] * 6, axis=1))
            l_s[n] += fold_sum(lifted)
            lifted = lifted.astype(BF)
            o_s[n] += dot_nn(lifted, values[g, p, :, heads(h)])
            probs[n, p] = lifted

    each(chip + 1, weigh)

    xs = []
    for g in range(NSEQ):
        outs = []
        x = []
        for h in range(2):
            n = 2 * g + h
            inv = 1.0 / jnp.sum(l_s[n], axis=1, keepdims=True)
            out = o_s[n] * inv
            outs.append(out.astype(BF))
            scaled = (g_s[g, :, heads(h)].astype(F32) * inv).astype(BF)
            delta = jnp.sum(scaled.astype(F32) * out, axis=1, keepdims=True)
            m_s[n] = jnp.broadcast_to(delta, (BLOCK, 128))
            g_s[g, :, heads(h)] = scaled
            mk = mt_ref[:, 256 + h * HD : 256 + (h + 1) * HD]
            mv = mt_ref[:, 512 + h * HD : 512 + (h + 1) * HD]
            x.append((dot_nt(mk, q_s[g, :, heads(h)]) * LN2).astype(BF))
            x.append(dot_nt(mv, scaled).astype(BF))
        xs.append(jnp.concatenate(x, axis=1))
        out_c = jnp.concatenate(outs, axis=1)
        back = jnp.where(rows == position(cols, offs[g]), 1.0, 0.0).astype(BF)
        out_ref[g] = dot_nn(back, out_c).astype(BF)
    zq[...] = jnp.zeros_like(zq)
    zt[...] = jnp.zeros_like(zt)

    def differentiate(p):
        for g in range(NSEQ):
            stack = []
            for h in range(2):
                n = 2 * g + h
                delta = jnp.concatenate([m_s[n]] * 6, axis=1)
                value = values[g, p, :, heads(h)]
                dp = dot_nt(g_s[g, 0:PATCHES, heads(h)], value)
                ds = (probs[n, p, 0:PATCHES, :].astype(F32) * (dp - delta[0:PATCHES])).astype(BF)
                dp_text = dot_nt(g_s[g, PATCHES:, heads(h)], value[0 : 2 * PATCHES])
                ds_text = (
                    probs[n, p, PATCHES:, 0 : 2 * PATCHES].astype(F32)
                    * (dp_text - delta[PATCHES:, 0 : 2 * PATCHES])
                ).astype(BF)
                zq[n] += dot_nn(ds, keys[g, p, :, heads(h)])
                stack += [ds[:, 0 : 2 * PATCHES], ds_text, probs[n, p, :, 0 : 2 * PATCHES]]
            zt[g, p] = dot_nn(xs[g], jnp.concatenate(stack, axis=0))

    each(chip + 1, differentiate)

    for g in range(NSEQ):
        own = jnp.zeros((PDIM, PATCHES), F32)
        for h in range(2):
            own = own + dot_nt(mt_ref[:, heads(h)], (zq[2 * g + h] * SCALE).astype(BF))
        for b in range(8):
            flat = zt[g, b // 2, :, PATCHES * (b % 2) : PATCHES * (b % 2 + 1)]
            flat = flat + jnp.where(seat == b, own, 0.0)
            dense = jnp.concatenate([flat[:, 64 * a : 64 * (a + 1)] for a in range(4)], axis=0).T
            z_ref[labels[g * 8 + b]] = dense.astype(BF)


def attend(seq, start, seat, same, other, qt, mt, grad):
    smem = pl.BlockSpec(memory_space=pltpu.SMEM)
    vmem = pl.BlockSpec(memory_space=pltpu.VMEM)
    return pl.pallas_call(
        attend_kernel,
        out_shape=(
            jax.ShapeDtypeStruct((NSEQ, BLOCK, 256), BF),
            jax.ShapeDtypeStruct((IMAGES, 64, 128), BF),
        ),
        in_specs=[smem] * 3 + [vmem] * 5,
        out_specs=(vmem,) * 2,
        scratch_shapes=[
            pltpu.SMEM((IMAGES,), jnp.int32),
            pltpu.VMEM((IMAGES, 64, 128), F32),
            pltpu.VMEM((512, 768), BF),
            pltpu.VMEM((NSEQ, 4, 2 * BLOCK, 256), BF),
            pltpu.VMEM((NSEQ, 4, 2 * BLOCK, 256), BF),
            pltpu.VMEM((4, 4, BLOCK, 2 * BLOCK), F32),
            pltpu.VMEM((4, 4, BLOCK, 2 * BLOCK), BF),
            pltpu.VMEM((NSEQ, BLOCK, 256), BF),
            pltpu.VMEM((NSEQ, BLOCK, 256), BF),
            pltpu.VMEM((4, BLOCK, HD), F32),
            pltpu.VMEM((4, BLOCK, 128), F32),
            pltpu.VMEM((4, BLOCK, 128), F32),
            pltpu.VMEM((NSEQ, 4, PDIM, 2 * PATCHES), F32),
            pltpu.VMEM((4, PATCHES, HD), F32),
        ],
        compiler_params=pltpu.CompilerParams(vmem_limit_bytes=52 * 2**20),
        name="attend",
    )(seq, start, seat, same, other, qt, mt, grad)


def finish_kernel(recv_ref, lat_ref, inv_ref, u_ref, out_ref):
    total = jnp.sum(recv_ref[...].astype(F32), axis=0)
    lat = lat_ref[...].astype(F32)
    for a in range(4):
        at = slice(8 * a, 8 * (a + 1))
        z = total[:, PDIM * a : PDIM * (a + 1)]
        inv = inv_ref[at, :][:, 0:1]
        inner = jnp.sum(lat[at] * z, axis=1, keepdims=True)
        out_ref[at, :] = inv * (z - u_ref[at, :] * (inv * inv * inner * (1.0 / D)))


def on_device(
    text_rows, latents, image_seq, image_start, norm_gain, w_patch, w_query, w_key, w_value, out_grad
):
    seats = lax.axis_size("seq")
    groups = lax.axis_size("dp")
    seat = lax.axis_index("seq").astype(jnp.int32).reshape(1)
    lat = latents.reshape(PDIM, PDIM)
    smem = pl.BlockSpec(memory_space=pltpu.SMEM)
    vmem = pl.BlockSpec(memory_space=pltpu.VMEM)
    hbm = pl.BlockSpec(memory_space=pltpu.HBM)
    send, inv, u = pl.pallas_call(
        pack_kernel,
        out_shape=(
            jax.ShapeDtypeStruct((groups, SEND_ROWS, 256), BF),
            jax.ShapeDtypeStruct((PDIM, 128), F32),
            jax.ShapeDtypeStruct((PDIM, PDIM), F32),
        ),
        in_specs=[hbm, hbm, smem, hbm, hbm, hbm],
        out_specs=(vmem,) * 3,
        scratch_shapes=[
            pltpu.SMEM((IMAGES,), jnp.int32),
            pltpu.SMEM((IMAGES,), jnp.int32),
            pltpu.VMEM((NSEQ, BLOCK, 256), BF),
            pltpu.VMEM((PDIM, PDIM), BF),
            pltpu.VMEM((PDIM, D), BF),
            pltpu.SemaphoreType.DMA((5,)),
        ],
        compiler_params=pltpu.CompilerParams(vmem_limit_bytes=32 * 2**20),
        name="pack",
    )(image_seq, image_start, seat, text_rows, lat, w_patch)
    recv = lax.all_to_all(send, "dp", 0, 0)

    qt, block, mt = pl.pallas_call(
        project_kernel,
        out_shape=(
            jax.ShapeDtypeStruct((NSEQ * TEXT, 256), BF),
            jax.ShapeDtypeStruct((KV_ROWS, 512), BF),
            jax.ShapeDtypeStruct((PDIM, 768), BF),
        ),
        in_specs=[vmem, vmem, vmem, hbm, vmem, vmem],
        out_specs=(vmem,) * 3,
        scratch_shapes=[
            pltpu.VMEM((NSEQ * TEXT + PDIM, D), BF),
            pltpu.VMEM((D, 256), BF),
            pltpu.SemaphoreType.DMA,
        ],
        compiler_params=pltpu.CompilerParams(vmem_limit_bytes=40 * 2**20),
        name="project",
    )(recv, w_query, w_key, w_value, w_patch, norm_gain.reshape(1, D))
    hops = [block] + [
        lax.ppermute(block, "seq", [(i, (i + 2 * k) % seats) for i in range(seats)])
        for k in range(1, seats // 2)
    ]
    same = jnp.stack(hops)
    other = lax.ppermute(same, "seq", [(i, i ^ 1) for i in range(seats)])

    attended, z = attend(image_seq, image_start, seat, same, other, qt, mt, out_grad)
    parts = lax.all_to_all(z.reshape(groups * seats, 8, 128), ("dp", "seq"), 0, 0)
    grad = pl.pallas_call(
        finish_kernel,
        out_shape=jax.ShapeDtypeStruct((PDIM, PDIM), F32),
        in_specs=[vmem] * 4,
        out_specs=vmem,
        compiler_params=pltpu.CompilerParams(vmem_limit_bytes=32 * 2**20),
        name="finish",
    )(parts, lat, inv, u)
    return (attended, grad.reshape(latents.shape))


def solution(mesh):
    in_specs = (
        P(None, "seq", "dp"),
        P("dp", "seq", None),
        P(),
        P(),
        P(),
        P(),
        P(None, "dp"),
        P(None, "dp"),
        P(None, "dp"),
        P(None, "seq", "dp"),
    )
    out_specs = (P(None, "seq", "dp"), P("dp", "seq", None))
    return jax.shard_map(
        on_device, mesh=mesh, in_specs=in_specs, out_specs=out_specs, check_vma=False
    )
```

```python
import functools
import math

import jax
import jax.numpy as jnp
from jax import lax
from jax.experimental import pallas as pl
from jax.experimental.pallas import tpu as pltpu
from jax.sharding import PartitionSpec as P

HD = 128
PATCHES = 256
PDIM = 32
BLOCK = 384
TEXT = BLOCK - PATCHES
IMAGES = 16
NSEQ = 2
D = 4096
epsilon = 1e-05
SCALE = HD ** (-0.5)
LN2 = math.log(2.0)
BF = jnp.bfloat16
F32 = jnp.float32
SEND_ROWS = NSEQ * TEXT + 16
KV_ROWS = NSEQ * TEXT + 32


def dot_nn(a, b):
    return lax.dot_general(a, b, (((1,), (0,)), ((), ())), preferred_element_type=F32)


def dot_nt(a, b):
    return lax.dot_general(a, b, (((1,), (1,)), ((), ())), preferred_element_type=F32)


def own_offsets(seq_ref, start_ref, seat):
    offs = [jnp.int32(0), jnp.int32(0)]
    for i in range(IMAGES):
        rel = start_ref[i] - seat * BLOCK
        mine = (rel >= 0) & (rel < BLOCK)
        for g in range(NSEQ):
            offs[g] = jnp.where(mine & (seq_ref[i] == g), rel, offs[g])
    return offs


def pack_kernel(
    seq_hbm, start_hbm, seat_ref, text_hbm, lat_hbm, wp_hbm,
    send_ref, inv_ref, u_ref,
    seq_ref, start_ref, text_ref, lat_ref, wp_ref, sems,
):
    pairs = (
        (seq_hbm, seq_ref), (start_hbm, start_ref), (lat_hbm, lat_ref), (wp_hbm, wp_ref),
        (text_hbm, text_ref),
    )
    copies = [pltpu.make_async_copy(a, b, sems.at[n]) for n, (a, b) in enumerate(pairs)]
    for copy in copies:
        copy.start()
    copies[2].wait()
    copies[3].wait()
    lat = lat_ref[...]
    wp = wp_ref[...]
    embedded = dot_nn(lat, wp).astype(BF)
    emb_f = embedded.astype(F32)
    inv = lax.rsqrt(jnp.sum(emb_f * emb_f, axis=1, keepdims=True) * (1.0 / D) + epsilon)
    inv_ref[...] = jnp.broadcast_to(inv, inv_ref.shape)
    u_ref[...] = dot_nt(embedded, wp)
    scaled = lat.astype(F32) * inv
    packed = jnp.concatenate([scaled[8 * a : 8 * (a + 1)] for a in range(4)], axis=1)
    tail = jnp.concatenate([packed, jnp.zeros((8, 128), F32)], axis=0)
    tail = jnp.concatenate([tail, jnp.zeros((16, 128), F32)], axis=1).astype(BF)
    copies[0].wait()
    copies[1].wait()
    offs = own_offsets(seq_ref, start_ref, seat_ref[0])
    copies[4].wait()
    row = lax.broadcasted_iota(jnp.int32, (TEXT, 256), 0)
    texts = []
    for g in range(NSEQ):
        low = text_ref[g, 0:TEXT, :].astype(F32)
        high = text_ref[g, PATCHES:BLOCK, :].astype(F32)
        texts.append(jnp.where(row < offs[g], low, high).astype(BF))
    for d in range(send_ref.shape[0]):
        for g in range(NSEQ):
            send_ref[d, g * TEXT : (g + 1) * TEXT, :] = texts[g]
        send_ref[d, NSEQ * TEXT :, :] = tail


def project_kernel(
    x_ref, wq_ref, wk_ref, wv_hbm, wp_ref, gain_ref, qt_ref, block_ref, mt_ref, left, wv_ref, sem
):
    copy = pltpu.make_async_copy(wv_hbm, wv_ref, sem)
    copy.start()
    rows = NSEQ * TEXT
    ssq = jnp.zeros((rows, 128), F32)
    tiles = []
    for d in range(x_ref.shape[0]):
        at = slice(256 * d, 256 * (d + 1))
        gain = gain_ref[:, at]
        x = x_ref[d, 0:rows, :].astype(F32)
        squares = x * x
        ssq = ssq + squares[:, :128] + squares[:, 128:]
        left[0:rows, at] = (x * gain).astype(BF)
        left[rows:, at] = (wp_ref[:, at].astype(F32) * gain).astype(BF)
        tiles.append(x_ref[d, rows : rows + 16, 0:128].astype(F32)[0:8])
    inv = lax.rsqrt(jnp.sum(ssq, axis=1, keepdims=True) * (1.0 / D) + epsilon)
    lat = [jnp.concatenate(tiles[4 * n : 4 * (n + 1)], axis=1) for n in range(4)]
    block_ref[rows:, :] = jnp.concatenate(lat, axis=0).astype(BF)
    query = dot_nn(left[...], wq_ref[...])
    qt_ref[...] = (query[0:rows] * (inv * (SCALE / LN2))).astype(BF)
    mt_ref[:, 0:256] = query[rows:].astype(BF)
    key = dot_nn(left[...], wk_ref[...])
    block_ref[0:rows, 0:256] = (key[0:rows] * inv).astype(BF)
    mt_ref[:, 256:512] = key[rows:].astype(BF)
    copy.wait()
    value = dot_nn(left[...], wv_ref[...])
    block_ref[0:rows, 256:512] = (value[0:rows] * inv).astype(BF)
    mt_ref[:, 512:768] = value[rows:].astype(BF)


def fold_max(s):
    return functools.reduce(jnp.maximum, [s[:, 128 * n : 128 * (n + 1)] for n in range(6)])


def fold_sum(s):
    return functools.reduce(jnp.add, [s[:, 128 * n : 128 * (n + 1)] for n in range(6)])


def position(index, offset):
    patch = 32 * ((index & 63) >> 3) + 8 * (index >> 6) + (index & 7)
    t = index - PATCHES
    return jnp.where(
        index < PATCHES, offset + patch, jnp.where(t < offset, t, t + PATCHES)
    )


def heads(h):
    return slice(h * HD, (h + 1) * HD)


def pinned(x):
    return pltpu.with_memory_space_constraint(x, pltpu.HBM)


CHAINS = [(g, h) for g in range(NSEQ) for h in range(2)]


def attend_kernel(
    seq_hbm, start_hbm, seat_ref, s0, s1, s2, s3, o0, o1, o2, o3, qt_ref, mt_ref, grad_hbm,
    out_ref, z_ref,
    labels, tiles, wide, keys, values, scores, probs, q_s, g_s, o_s, m_s, l_s, zt, zq, grad_ref, seq_ref, start_ref, sems,
):
    pairs = ((seq_hbm, seq_ref), (start_hbm, start_ref), (grad_hbm, grad_ref))
    copies = [pltpu.make_async_copy(a, b, sems.at[n]) for n, (a, b) in enumerate(pairs)]
    for copy in copies:
        copy.start()
    seat = seat_ref[0]
    chip, core = seat >> 1, seat & 1
    wide[...] = jnp.zeros_like(wide)
    for a in range(4):
        wide[128 * a + PDIM * a : 128 * a + PDIM * (a + 1), :] = mt_ref[...]
    for k in range(4):
        pair = (chip - k) & 3
        for ref, parity in (((s0, s1, s2, s3)[k], core), ((o0, o1, o2, o3)[k], 1 - core)):
            part = ref[NSEQ * TEXT :, :].astype(F32)
            at = pl.multiple_of((2 * pair + parity) * 8, 8)
            for i in range(IMAGES):
                tiles[i, pl.ds(at, 8), :] = part[
                    8 * (i // 4) : 8 * (i // 4 + 1), 128 * (i % 4) : 128 * (i % 4 + 1)
                ]
            at = pl.ds(pl.multiple_of(2 * PATCHES + TEXT * parity, TEXT), TEXT)
            for g in range(NSEQ):
                keys[g, pair, at, :] = ref[g * TEXT : (g + 1) * TEXT, 0:256]
                values[g, pair, at, :] = ref[g * TEXT : (g + 1) * TEXT, 256:512]

    copies[0].wait()
    copies[1].wait()
    offs = own_offsets(seq_ref, start_ref, seat)
    for i in range(IMAGES):
        labels[seq_ref[i] * 8 + lax.div(start_ref[i], BLOCK)] = i
    rows = lax.broadcasted_iota(jnp.int32, (BLOCK, BLOCK), 0)
    cols = lax.broadcasted_iota(jnp.int32, (BLOCK, BLOCK), 1)
    for g in range(NSEQ):
        own_tile = tiles[labels[g * 8 + seat]].astype(BF)
        in_order = jnp.concatenate([tiles[labels[g * 8 + b]] for b in range(8)], axis=0).astype(BF)
        for a in range(4):
            patch = wide[128 * a : 128 * (a + 1), :]
            q_s[g, 64 * a : 64 * (a + 1), :] = (
                dot_nn(own_tile, patch[:, 0:256]) * (SCALE / LN2)
            ).astype(BF)
            kv = dot_nn(in_order, patch[:, 256:768]).astype(BF)
            for b in range(8):
                at = slice(PATCHES * (b % 2) + 64 * a, PATCHES * (b % 2) + 64 * (a + 1))
                keys[g, b // 2, at, :] = kv[64 * b : 64 * (b + 1), 0:256]
                values[g, b // 2, at, :] = kv[64 * b : 64 * (b + 1), 256:512]
        q_s[g, PATCHES:, :] = qt_ref[g * TEXT : (g + 1) * TEXT, :]
    copies[2].wait()
    for g in range(NSEQ):
        place = jnp.where(cols == position(rows, offs[g]), 1.0, 0.0).astype(BF)
        g_s[g] = dot_nn(place, grad_ref[g]).astype(BF)

    def each(count, body):
        def step(p, carry):
            body(p)
            return carry

        lax.fori_loop(0, count, step, 0)

    q_row = lax.broadcasted_iota(jnp.int32, (BLOCK, 2 * BLOCK), 0)
    k_col = lax.broadcasted_iota(jnp.int32, (BLOCK, 2 * BLOCK), 1)
    in_image = k_col < 2 * PATCHES
    second = jnp.where(in_image, k_col >> 8, (k_col - 2 * PATCHES) >> 7)
    k_row = jnp.where(in_image, k_col & (PATCHES - 1), PATCHES + (k_col & (TEXT - 1)))

    def score(p, diagonal=False):
        for n, (g, h) in enumerate(CHAINS):
            s = dot_nt(q_s[g, :, heads(h)], keys[g, p, :, heads(h)])
            if diagonal:
                off = offs[g]
                reach = jnp.where(q_row < PATCHES, off + (PATCHES - 1), position(q_row, off))
                place = position(k_row, off) + BLOCK * (second - core)
                s = jnp.where(place <= reach, s, -jnp.inf)
                m_s[n] = fold_max(s)
            else:
                m_s[n] = jnp.maximum(m_s[n], fold_max(s))
            scores[n, p] = s

    score(chip, True)
    each(chip, score)

    o_s[...] = jnp.zeros_like(o_s)
    l_s[...] = jnp.zeros_like(l_s)
    for n in range(4):
        m_s[n] = jnp.broadcast_to(jnp.max(m_s[n], axis=1, keepdims=True), (BLOCK, 128))

    def weigh(p):
        for n, (g, h) in enumerate(CHAINS):
            top = m_s[n]
            lifted = jnp.exp2(scores[n, p] - jnp.concatenate([top] * 6, axis=1))
            l_s[n] += fold_sum(lifted)
            lifted = lifted.astype(BF)
            o_s[n] += dot_nn(lifted, values[g, p, :, heads(h)])
            probs[n, p] = lifted

    each(chip + 1, weigh)

    xs = []
    for g in range(NSEQ):
        outs = []
        x = []
        for h in range(2):
            n = 2 * g + h
            inv = 1.0 / jnp.sum(l_s[n], axis=1, keepdims=True)
            out = o_s[n] * inv
            outs.append(out.astype(BF))
            scaled = (g_s[g, :, heads(h)].astype(F32) * inv).astype(BF)
            delta = jnp.sum(scaled.astype(F32) * out, axis=1, keepdims=True)
            m_s[n] = jnp.broadcast_to(delta, (BLOCK, 128))
            g_s[g, :, heads(h)] = scaled
            mk = mt_ref[:, 256 + h * HD : 256 + (h + 1) * HD]
            mv = mt_ref[:, 512 + h * HD : 512 + (h + 1) * HD]
            x.append((dot_nt(mk, q_s[g, :, heads(h)]) * LN2).astype(BF))
            x.append(dot_nt(mv, scaled).astype(BF))
        xs.append(jnp.concatenate(x, axis=1))
        out_c = jnp.concatenate(outs, axis=1)
        back = jnp.where(rows == position(cols, offs[g]), 1.0, 0.0).astype(BF)
        out_ref[g] = dot_nn(back, out_c).astype(BF)
    zq[...] = jnp.zeros_like(zq)
    zt[...] = jnp.zeros_like(zt)

    def differentiate(p):
        for g in range(NSEQ):
            stack = []
            for h in range(2):
                n = 2 * g + h
                delta = jnp.concatenate([m_s[n]] * 6, axis=1)
                value = values[g, p, :, heads(h)]
                dp = dot_nt(g_s[g, 0:PATCHES, heads(h)], value)
                ds = (probs[n, p, 0:PATCHES, :].astype(F32) * (dp - delta[0:PATCHES])).astype(BF)
                dp_text = dot_nt(g_s[g, PATCHES:, heads(h)], value[0 : 2 * PATCHES])
                ds_text = (
                    probs[n, p, PATCHES:, 0 : 2 * PATCHES].astype(F32)
                    * (dp_text - delta[PATCHES:, 0 : 2 * PATCHES])
                ).astype(BF)
                zq[n] += dot_nn(ds, keys[g, p, :, heads(h)])
                stack += [ds[:, 0 : 2 * PATCHES], ds_text, probs[n, p, :, 0 : 2 * PATCHES]]
            zt[g, p] = dot_nn(xs[g], jnp.concatenate(stack, axis=0))

    each(chip + 1, differentiate)

    for g in range(NSEQ):
        own = jnp.zeros((PDIM, PATCHES), F32)
        for h in range(2):
            own = own + dot_nt(mt_ref[:, heads(h)], (zq[2 * g + h] * SCALE).astype(BF))
        for b in range(8):
            flat = zt[g, b // 2, :, PATCHES * (b % 2) : PATCHES * (b % 2 + 1)]
            flat = flat + jnp.where(seat == b, own, 0.0)
            dense = jnp.concatenate([flat[:, 64 * a : 64 * (a + 1)] for a in range(4)], axis=0).T
            z_ref[labels[g * 8 + b]] = dense.astype(BF)


def attend(seq, start, seat, same, other, qt, mt, grad):
    hbm = pl.BlockSpec(memory_space=pltpu.HBM)
    smem = pl.BlockSpec(memory_space=pltpu.SMEM)
    vmem = pl.BlockSpec(memory_space=pltpu.VMEM)
    return pl.pallas_call(
        attend_kernel,
        out_shape=(
            jax.ShapeDtypeStruct((NSEQ, BLOCK, 256), BF),
            jax.ShapeDtypeStruct((IMAGES, 64, 128), BF),
        ),
        in_specs=[hbm, hbm, smem] + [vmem] * 10 + [hbm],
        out_specs=(vmem,) * 2,
        scratch_shapes=[
            pltpu.SMEM((IMAGES,), jnp.int32),
            pltpu.VMEM((IMAGES, 64, 128), F32),
            pltpu.VMEM((512, 768), BF),
            pltpu.VMEM((NSEQ, 4, 2 * BLOCK, 256), BF),
            pltpu.VMEM((NSEQ, 4, 2 * BLOCK, 256), BF),
            pltpu.VMEM((4, 4, BLOCK, 2 * BLOCK), F32),
            pltpu.VMEM((4, 4, BLOCK, 2 * BLOCK), BF),
            pltpu.VMEM((NSEQ, BLOCK, 256), BF),
            pltpu.VMEM((NSEQ, BLOCK, 256), BF),
            pltpu.VMEM((4, BLOCK, HD), F32),
            pltpu.VMEM((4, BLOCK, 128), F32),
            pltpu.VMEM((4, BLOCK, 128), F32),
            pltpu.VMEM((NSEQ, 4, PDIM, 2 * PATCHES), F32),
            pltpu.VMEM((4, PATCHES, HD), F32),
            pltpu.VMEM((NSEQ, BLOCK, 256), BF),
            pltpu.SMEM((IMAGES,), jnp.int32),
            pltpu.SMEM((IMAGES,), jnp.int32),
            pltpu.SemaphoreType.DMA((3,)),
        ],
        compiler_params=pltpu.CompilerParams(vmem_limit_bytes=52 * 2**20),
        name="attend",
    )(pinned(seq), pinned(start), seat, *same, *other, qt, mt, pinned(grad))


def finish_kernel(recv_ref, lat_ref, inv_ref, u_ref, out_ref):
    total = jnp.sum(recv_ref[...].astype(F32), axis=0)
    lat = lat_ref[...].astype(F32)
    for a in range(4):
        at = slice(8 * a, 8 * (a + 1))
        z = total[:, PDIM * a : PDIM * (a + 1)]
        inv = inv_ref[at, :][:, 0:1]
        inner = jnp.sum(lat[at] * z, axis=1, keepdims=True)
        out_ref[at, :] = inv * (z - u_ref[at, :] * (inv * inv * inner * (1.0 / D)))


def on_device(
    text_rows, latents, image_seq, image_start, norm_gain, w_patch, w_query, w_key, w_value, out_grad
):
    seats = lax.axis_size("seq")
    groups = lax.axis_size("dp")
    seat = lax.axis_index("seq").astype(jnp.int32).reshape(1)
    lat = latents.reshape(PDIM, PDIM)
    smem = pl.BlockSpec(memory_space=pltpu.SMEM)
    vmem = pl.BlockSpec(memory_space=pltpu.VMEM)
    hbm = pl.BlockSpec(memory_space=pltpu.HBM)
    send, inv, u = pl.pallas_call(
        pack_kernel,
        out_shape=(
            jax.ShapeDtypeStruct((groups, SEND_ROWS, 256), BF),
            jax.ShapeDtypeStruct((PDIM, 128), F32),
            jax.ShapeDtypeStruct((PDIM, PDIM), F32),
        ),
        in_specs=[hbm, hbm, smem, hbm, hbm, hbm],
        out_specs=(vmem,) * 3,
        scratch_shapes=[
            pltpu.SMEM((IMAGES,), jnp.int32),
            pltpu.SMEM((IMAGES,), jnp.int32),
            pltpu.VMEM((NSEQ, BLOCK, 256), BF),
            pltpu.VMEM((PDIM, PDIM), BF),
            pltpu.VMEM((PDIM, D), BF),
            pltpu.SemaphoreType.DMA((5,)),
        ],
        compiler_params=pltpu.CompilerParams(vmem_limit_bytes=32 * 2**20),
        name="pack",
    )(pinned(image_seq), pinned(image_start), seat, pinned(text_rows), pinned(lat), pinned(w_patch))
    recv = lax.all_to_all(send, "dp", 0, 0)

    qt, block, mt = pl.pallas_call(
        project_kernel,
        out_shape=(
            jax.ShapeDtypeStruct((NSEQ * TEXT, 256), BF),
            jax.ShapeDtypeStruct((KV_ROWS, 512), BF),
            jax.ShapeDtypeStruct((PDIM, 768), BF),
        ),
        in_specs=[vmem, vmem, vmem, hbm, vmem, vmem],
        out_specs=(vmem,) * 3,
        scratch_shapes=[
            pltpu.VMEM((NSEQ * TEXT + PDIM, D), BF),
            pltpu.VMEM((D, 256), BF),
            pltpu.SemaphoreType.DMA,
        ],
        compiler_params=pltpu.CompilerParams(vmem_limit_bytes=40 * 2**20),
        name="project",
    )(recv, w_query, w_key, pinned(w_value), w_patch, norm_gain.reshape(1, D))
    hops = [block] + [
        lax.ppermute(block, "seq", [(i, (i + 2 * k) % seats) for i in range(seats)])
        for k in range(1, seats // 2)
    ]
    other = [lax.ppermute(hop, "seq", [(i, i ^ 1) for i in range(seats)]) for hop in hops]
    attended, z = attend(image_seq, image_start, seat, hops, other, qt, mt, out_grad)
    parts = lax.all_to_all(z.reshape(groups * seats, 8, 128), ("dp", "seq"), 0, 0)
    grad = pl.pallas_call(
        finish_kernel,
        out_shape=jax.ShapeDtypeStruct((PDIM, PDIM), F32),
        in_specs=[vmem] * 4,
        out_specs=vmem,
        compiler_params=pltpu.CompilerParams(vmem_limit_bytes=32 * 2**20),
        name="finish",
    )(parts, lat, inv, u)
    return (attended, grad.reshape(latents.shape))


def solution(mesh):
    in_specs = (
        P(None, "seq", "dp"),
        P("dp", "seq", None),
        P(),
        P(),
        P(),
        P(),
        P(None, "dp"),
        P(None, "dp"),
        P(None, "dp"),
        P(None, "seq", "dp"),
    )
    out_specs = (P(None, "seq", "dp"), P("dp", "seq", None))
    return jax.shard_map(
        on_device, mesh=mesh, in_specs=in_specs, out_specs=out_specs, check_vma=False
    )
```

```python
import functools
import math

import jax
import jax.numpy as jnp
from jax import lax
from jax.experimental import pallas as pl
from jax.experimental.pallas import tpu as pltpu
from jax.sharding import PartitionSpec as P

HD = 128
PATCHES = 256
PDIM = 32
BLOCK = 384
TEXT = BLOCK - PATCHES
IMAGES = 16
NSEQ = 2
D = 4096
epsilon = 1e-05
SCALE = HD ** (-0.5)
LN2 = math.log(2.0)
BF = jnp.bfloat16
F32 = jnp.float32
SIDE = 4
HOPS = (1, 3, 2)
KV_ROWS = NSEQ * TEXT + 32


def dot_nn(a, b):
    return lax.dot_general(a, b, (((1,), (0,)), ((), ())), preferred_element_type=F32)


def dot_nt(a, b):
    return lax.dot_general(a, b, (((1,), (1,)), ((), ())), preferred_element_type=F32)


def own_offsets(seq_ref, start_ref, seat):
    offs = [jnp.int32(0), jnp.int32(0)]
    for i in range(IMAGES):
        rel = start_ref[i] - seat * BLOCK
        mine = (rel >= 0) & (rel < BLOCK)
        for g in range(NSEQ):
            offs[g] = jnp.where(mine & (seq_ref[i] == g), rel, offs[g])
    return offs


def pack_kernel(
    seq_hbm, start_hbm, seat_ref, text_hbm, lat_hbm, wp_hbm, gain_hbm,
    first_ref, second_ref, inv_ref, u_ref, patch_ref, gain_ref,
    seq_ref, start_ref, text_ref, lat_ref, wp_ref, sems,
):
    pairs = (
        (seq_hbm, seq_ref), (start_hbm, start_ref), (lat_hbm, lat_ref), (wp_hbm, wp_ref),
        (text_hbm, text_ref), (gain_hbm, gain_ref),
    )
    copies = [pltpu.make_async_copy(a, b, sems.at[n]) for n, (a, b) in enumerate(pairs)]
    for copy in copies:
        copy.start()
    copies[2].wait()
    copies[3].wait()
    lat = lat_ref[...]
    wp = wp_ref[...]
    embedded = dot_nn(lat, wp).astype(BF)
    emb_f = embedded.astype(F32)
    inv = lax.rsqrt(jnp.sum(emb_f * emb_f, axis=1, keepdims=True) * (1.0 / D) + epsilon)
    inv_ref[...] = jnp.broadcast_to(inv, inv_ref.shape)
    u_ref[...] = dot_nt(embedded, wp)
    scaled = lat.astype(F32) * inv
    packed = jnp.concatenate([scaled[8 * a : 8 * (a + 1)] for a in range(4)], axis=1)
    tail = jnp.concatenate([packed, jnp.zeros((8, 128), F32)], axis=0)
    tail = jnp.concatenate([tail, jnp.zeros((16, 128), F32)], axis=1).astype(BF)
    copies[0].wait()
    copies[1].wait()
    offs = own_offsets(seq_ref, start_ref, seat_ref[0])
    copies[4].wait()
    row = lax.broadcasted_iota(jnp.int32, (TEXT, 256), 0)
    for g, ref in ((0, first_ref), (1, second_ref)):
        low = text_ref[g, 0:TEXT, :].astype(F32)
        high = text_ref[g, PATCHES:BLOCK, :].astype(F32)
        ref[0:TEXT, :] = jnp.where(row < offs[g], low, high).astype(BF)
    first_ref[TEXT:, :] = tail
    second_ref[TEXT:, :] = jnp.zeros((16, 256), BF)
    copies[5].wait()
    patch_ref[...] = (wp.astype(F32) * gain_ref[...]).astype(BF)


def fold_kernel(patch_ref, wq_hbm, wk_hbm, wv_hbm, wq_ref, wk_ref, wv_ref, mt_ref, sems):
    pairs = ((wq_hbm, wq_ref), (wk_hbm, wk_ref), (wv_hbm, wv_ref))
    copies = [pltpu.make_async_copy(a, b, sems.at[n]) for n, (a, b) in enumerate(pairs)]
    for copy in copies:
        copy.start()
    for n, (_, ref) in enumerate(pairs):
        copies[n].wait()
        mt_ref[:, 256 * n : 256 * (n + 1)] = dot_nn(patch_ref[...], ref[...]).astype(BF)


def project_kernel(
    group_ref, f0, f1, f2, f3, t0, t1, t2, t3, gain_ref, wq_ref, wk_ref, wv_ref,
    qt_ref, block_ref,
    left, lat,
):
    rows = NSEQ * TEXT
    z_here, y_here = group_ref[0] >> 2, group_ref[0] & 3
    sums = [jnp.zeros((TEXT, 128), F32) for g in range(NSEQ)]

    def place(ref, piece, g, z, y):
        at = pl.ds(pl.multiple_of(256 * (SIDE * z + y), 256), 256)
        x = ref[piece, 0:TEXT, :].astype(F32)
        left[g * TEXT : (g + 1) * TEXT, at] = (x * gain_ref[:, at]).astype(BF)
        squares = x * x
        sums[g] = sums[g] + squares[:, :128] + squares[:, 128:]

    for n, far in enumerate((0,) + HOPS):
        for m, near in enumerate((0,) + HOPS):
            ref, z, y = (f0, f1, f2, f3)[n], (z_here - far) & 3, (y_here - near) & 3
            place(ref, m, 0, z, y)
            tile = ref[m, TEXT : TEXT + 16, 0:128].astype(F32)[0:8]
            lat[pl.ds(pl.multiple_of(8 * z, 8), 8), pl.ds(pl.multiple_of(128 * y, 128), 128)] = tile
            place((t0, t1, t2, t3)[n], m, 1, (z_here - near) & 3, (y_here - far) & 3)
    ssq = jnp.concatenate(sums, axis=0)
    inv = lax.rsqrt(jnp.sum(ssq, axis=1, keepdims=True) * (1.0 / D) + epsilon)
    block_ref[rows:, :] = lat[...].astype(BF)
    query = dot_nn(left[...], wq_ref[...])
    qt_ref[...] = (query * (inv * (SCALE / LN2))).astype(BF)
    key = dot_nn(left[...], wk_ref[...])
    block_ref[0:rows, 0:256] = (key * inv).astype(BF)
    value = dot_nn(left[...], wv_ref[...])
    block_ref[0:rows, 256:512] = (value * inv).astype(BF)


def fold_max(s):
    return functools.reduce(jnp.maximum, [s[:, 128 * n : 128 * (n + 1)] for n in range(6)])


def fold_sum(s):
    return functools.reduce(jnp.add, [s[:, 128 * n : 128 * (n + 1)] for n in range(6)])


def position(index, offset):
    patch = 32 * ((index & 63) >> 3) + 8 * (index >> 6) + (index & 7)
    t = index - PATCHES
    return jnp.where(
        index < PATCHES, offset + patch, jnp.where(t < offset, t, t + PATCHES)
    )


def heads(h):
    return slice(h * HD, (h + 1) * HD)


def pinned(x):
    return pltpu.with_memory_space_constraint(x, pltpu.HBM)


CHAINS = [(g, h) for g in range(NSEQ) for h in range(2)]


def attend_kernel(
    seq_hbm, start_hbm, seat_ref, s0, s1, s2, s3, o0, o1, o2, o3, qt_ref, mt_ref, grad_hbm,
    out_ref, z_ref,
    labels, tiles, wide, keys, values, scores, probs, q_s, g_s, o_s, m_s, l_s, zt, zq, grad_ref, seq_ref, start_ref, sems,
):
    pairs = ((seq_hbm, seq_ref), (start_hbm, start_ref), (grad_hbm, grad_ref))
    copies = [pltpu.make_async_copy(a, b, sems.at[n]) for n, (a, b) in enumerate(pairs)]
    for copy in copies:
        copy.start()
    seat = seat_ref[0]
    chip, core = seat >> 1, seat & 1
    wide[...] = jnp.zeros_like(wide)
    for a in range(4):
        wide[128 * a + PDIM * a : 128 * a + PDIM * (a + 1), :] = mt_ref[...]
    for k in range(4):
        pair = (chip - k) & 3
        for ref, parity in (((s0, s1, s2, s3)[k], core), ((o0, o1, o2, o3)[k], 1 - core)):
            part = ref[NSEQ * TEXT :, :].astype(F32)
            at = pl.multiple_of((2 * pair + parity) * 8, 8)
            for i in range(IMAGES):
                tiles[i, pl.ds(at, 8), :] = part[
                    8 * (i // 4) : 8 * (i // 4 + 1), 128 * (i % 4) : 128 * (i % 4 + 1)
                ]
            at = pl.ds(pl.multiple_of(2 * PATCHES + TEXT * parity, TEXT), TEXT)
            for g in range(NSEQ):
                keys[g, pair, at, :] = ref[g * TEXT : (g + 1) * TEXT, 0:256]
                values[g, pair, at, :] = ref[g * TEXT : (g + 1) * TEXT, 256:512]

    copies[0].wait()
    copies[1].wait()
    offs = own_offsets(seq_ref, start_ref, seat)
    for i in range(IMAGES):
        labels[seq_ref[i] * 8 + lax.div(start_ref[i], BLOCK)] = i
    rows = lax.broadcasted_iota(jnp.int32, (BLOCK, BLOCK), 0)
    cols = lax.broadcasted_iota(jnp.int32, (BLOCK, BLOCK), 1)
    for g in range(NSEQ):
        own_tile = tiles[labels[g * 8 + seat]].astype(BF)
        in_order = jnp.concatenate([tiles[labels[g * 8 + b]] for b in range(8)], axis=0).astype(BF)
        for a in range(4):
            patch = wide[128 * a : 128 * (a + 1), :]
            q_s[g, 64 * a : 64 * (a + 1), :] = (
                dot_nn(own_tile, patch[:, 0:256]) * (SCALE / LN2)
            ).astype(BF)
            kv = dot_nn(in_order, patch[:, 256:768]).astype(BF)
            for b in range(8):
                at = slice(PATCHES * (b % 2) + 64 * a, PATCHES * (b % 2) + 64 * (a + 1))
                keys[g, b // 2, at, :] = kv[64 * b : 64 * (b + 1), 0:256]
                values[g, b // 2, at, :] = kv[64 * b : 64 * (b + 1), 256:512]
        q_s[g, PATCHES:, :] = qt_ref[g * TEXT : (g + 1) * TEXT, :]
    copies[2].wait()
    for g in range(NSEQ):
        place = jnp.where(cols == position(rows, offs[g]), 1.0, 0.0).astype(BF)
        g_s[g] = dot_nn(place, grad_ref[g]).astype(BF)

    def each(count, body):
        def step(p, carry):
            body(p)
            return carry

        lax.fori_loop(0, count, step, 0)

    q_row = lax.broadcasted_iota(jnp.int32, (BLOCK, 2 * BLOCK), 0)
    k_col = lax.broadcasted_iota(jnp.int32, (BLOCK, 2 * BLOCK), 1)
    in_image = k_col < 2 * PATCHES
    second = jnp.where(in_image, k_col >> 8, (k_col - 2 * PATCHES) >> 7)
    k_row = jnp.where(in_image, k_col & (PATCHES - 1), PATCHES + (k_col & (TEXT - 1)))

    def score(p, diagonal=False):
        for n, (g, h) in enumerate(CHAINS):
            s = dot_nt(q_s[g, :, heads(h)], keys[g, p, :, heads(h)])
            if diagonal:
                off = offs[g]
                reach = jnp.where(q_row < PATCHES, off + (PATCHES - 1), position(q_row, off))
                place = position(k_row, off) + BLOCK * (second - core)
                s = jnp.where(place <= reach, s, -jnp.inf)
                m_s[n] = fold_max(s)
            else:
                m_s[n] = jnp.maximum(m_s[n], fold_max(s))
            scores[n, p] = s

    score(chip, True)
    each(chip, score)

    o_s[...] = jnp.zeros_like(o_s)
    l_s[...] = jnp.zeros_like(l_s)
    for n in range(4):
        m_s[n] = jnp.broadcast_to(jnp.max(m_s[n], axis=1, keepdims=True), (BLOCK, 128))

    def weigh(p):
        for n, (g, h) in enumerate(CHAINS):
            top = m_s[n]
            lifted = jnp.exp2(scores[n, p] - jnp.concatenate([top] * 6, axis=1))
            l_s[n] += fold_sum(lifted)
            lifted = lifted.astype(BF)
            o_s[n] += dot_nn(lifted, values[g, p, :, heads(h)])
            probs[n, p] = lifted

    each(chip + 1, weigh)

    xs = []
    for g in range(NSEQ):
        outs = []
        x = []
        for h in range(2):
            n = 2 * g + h
            inv = 1.0 / jnp.sum(l_s[n], axis=1, keepdims=True)
            out = o_s[n] * inv
            outs.append(out.astype(BF))
            scaled = (g_s[g, :, heads(h)].astype(F32) * inv).astype(BF)
            delta = jnp.sum(scaled.astype(F32) * out, axis=1, keepdims=True)
            m_s[n] = jnp.broadcast_to(delta, (BLOCK, 128))
            g_s[g, :, heads(h)] = scaled
            mk = mt_ref[:, 256 + h * HD : 256 + (h + 1) * HD]
            mv = mt_ref[:, 512 + h * HD : 512 + (h + 1) * HD]
            x.append((dot_nt(mk, q_s[g, :, heads(h)]) * LN2).astype(BF))
            x.append(dot_nt(mv, scaled).astype(BF))
        xs.append(jnp.concatenate(x, axis=1))
        out_c = jnp.concatenate(outs, axis=1)
        back = jnp.where(rows == position(cols, offs[g]), 1.0, 0.0).astype(BF)
        out_ref[g] = dot_nn(back, out_c).astype(BF)
    zq[...] = jnp.zeros_like(zq)
    zt[...] = jnp.zeros_like(zt)

    def differentiate(p):
        for g in range(NSEQ):
            stack = []
            for h in range(2):
                n = 2 * g + h
                delta = jnp.concatenate([m_s[n]] * 6, axis=1)
                value = values[g, p, :, heads(h)]
                dp = dot_nt(g_s[g, 0:PATCHES, heads(h)], value)
                ds = (probs[n, p, 0:PATCHES, :].astype(F32) * (dp - delta[0:PATCHES])).astype(BF)
                dp_text = dot_nt(g_s[g, PATCHES:, heads(h)], value[0 : 2 * PATCHES])
                ds_text = (
                    probs[n, p, PATCHES:, 0 : 2 * PATCHES].astype(F32)
                    * (dp_text - delta[PATCHES:, 0 : 2 * PATCHES])
                ).astype(BF)
                zq[n] += dot_nn(ds, keys[g, p, :, heads(h)])
                stack += [ds[:, 0 : 2 * PATCHES], ds_text, probs[n, p, :, 0 : 2 * PATCHES]]
            zt[g, p] = dot_nn(xs[g], jnp.concatenate(stack, axis=0))

    each(chip + 1, differentiate)

    for g in range(NSEQ):
        own = jnp.zeros((PDIM, PATCHES), F32)
        for h in range(2):
            own = own + dot_nt(mt_ref[:, heads(h)], (zq[2 * g + h] * SCALE).astype(BF))
        for b in range(8):
            flat = zt[g, b // 2, :, PATCHES * (b % 2) : PATCHES * (b % 2 + 1)]
            flat = flat + jnp.where(seat == b, own, 0.0)
            dense = jnp.concatenate([flat[:, 64 * a : 64 * (a + 1)] for a in range(4)], axis=0).T
            z_ref[labels[g * 8 + b]] = dense.astype(BF)


def attend(seq, start, seat, same, other, qt, mt, grad):
    hbm = pl.BlockSpec(memory_space=pltpu.HBM)
    smem = pl.BlockSpec(memory_space=pltpu.SMEM)
    vmem = pl.BlockSpec(memory_space=pltpu.VMEM)
    return pl.pallas_call(
        attend_kernel,
        out_shape=(
            jax.ShapeDtypeStruct((NSEQ, BLOCK, 256), BF),
            jax.ShapeDtypeStruct((IMAGES, 64, 128), BF),
        ),
        in_specs=[hbm, hbm, smem] + [vmem] * 10 + [hbm],
        out_specs=(vmem,) * 2,
        scratch_shapes=[
            pltpu.SMEM((IMAGES,), jnp.int32),
            pltpu.VMEM((IMAGES, 64, 128), F32),
            pltpu.VMEM((512, 768), BF),
            pltpu.VMEM((NSEQ, 4, 2 * BLOCK, 256), BF),
            pltpu.VMEM((NSEQ, 4, 2 * BLOCK, 256), BF),
            pltpu.VMEM((4, 4, BLOCK, 2 * BLOCK), F32),
            pltpu.VMEM((4, 4, BLOCK, 2 * BLOCK), BF),
            pltpu.VMEM((NSEQ, BLOCK, 256), BF),
            pltpu.VMEM((NSEQ, BLOCK, 256), BF),
            pltpu.VMEM((4, BLOCK, HD), F32),
            pltpu.VMEM((4, BLOCK, 128), F32),
            pltpu.VMEM((4, BLOCK, 128), F32),
            pltpu.VMEM((NSEQ, 4, PDIM, 2 * PATCHES), F32),
            pltpu.VMEM((4, PATCHES, HD), F32),
            pltpu.VMEM((NSEQ, BLOCK, 256), BF),
            pltpu.SMEM((IMAGES,), jnp.int32),
            pltpu.SMEM((IMAGES,), jnp.int32),
            pltpu.SemaphoreType.DMA((3,)),
        ],
        compiler_params=pltpu.CompilerParams(vmem_limit_bytes=52 * 2**20),
        name="attend",
    )(pinned(seq), pinned(start), seat, *same, *other, qt, mt, pinned(grad))


def finish_kernel(recv_ref, lat_ref, inv_ref, u_ref, out_ref):
    total = jnp.sum(recv_ref[...].astype(F32), axis=0)
    lat = lat_ref[...].astype(F32)
    for a in range(4):
        at = slice(8 * a, 8 * (a + 1))
        z = total[:, PDIM * a : PDIM * (a + 1)]
        inv = inv_ref[at, :][:, 0:1]
        inner = jnp.sum(lat[at] * z, axis=1, keepdims=True)
        out_ref[at, :] = inv * (z - u_ref[at, :] * (inv * inv * inner * (1.0 / D)))


def on_device(
    text_rows, latents, image_seq, image_start, norm_gain, w_patch, w_query, w_key, w_value, out_grad
):
    seats = lax.axis_size("seq")
    groups = lax.axis_size("dp")
    seat = lax.axis_index("seq").astype(jnp.int32).reshape(1)
    group = lax.axis_index("dp").astype(jnp.int32).reshape(1)
    side = SIDE
    assert groups == side * side

    def shift_y(x, k):
        pairs = [(i, i // side * side + (i + k) % side) for i in range(groups)]
        return lax.ppermute(x, "dp", pairs)

    def shift_z(x, k):
        return lax.ppermute(x, "dp", [(i, (i + side * k) % groups) for i in range(groups)])

    lat = latents.reshape(PDIM, PDIM)
    smem = pl.BlockSpec(memory_space=pltpu.SMEM)
    vmem = pl.BlockSpec(memory_space=pltpu.VMEM)
    hbm = pl.BlockSpec(memory_space=pltpu.HBM)
    first, second, inv, u, patch, gain = pl.pallas_call(
        pack_kernel,
        out_shape=(
            jax.ShapeDtypeStruct((TEXT + 16, 256), BF),
            jax.ShapeDtypeStruct((TEXT + 16, 256), BF),
            jax.ShapeDtypeStruct((PDIM, 128), F32),
            jax.ShapeDtypeStruct((PDIM, PDIM), F32),
            jax.ShapeDtypeStruct((PDIM, D), BF),
            jax.ShapeDtypeStruct((1, D), F32),
        ),
        in_specs=[hbm, hbm, smem, hbm, hbm, hbm, hbm],
        out_specs=(vmem,) * 6,
        scratch_shapes=[
            pltpu.SMEM((IMAGES,), jnp.int32),
            pltpu.SMEM((IMAGES,), jnp.int32),
            pltpu.VMEM((NSEQ, BLOCK, 256), BF),
            pltpu.VMEM((PDIM, PDIM), BF),
            pltpu.VMEM((PDIM, D), BF),
            pltpu.SemaphoreType.DMA((6,)),
        ],
        compiler_params=pltpu.CompilerParams(vmem_limit_bytes=32 * 2**20),
        name="pack",
    )(
        pinned(image_seq), pinned(image_start), seat, pinned(text_rows), pinned(lat), pinned(w_patch),
        pinned(norm_gain.reshape(1, D)),
    )
    near = []
    for k in HOPS:
        near += [shift_y(first, k), shift_z(second, k)]
    near = lax.optimization_barrier(tuple(near))
    first_y, second_z = lax.optimization_barrier(
        (jnp.stack((first,) + near[0::2]), jnp.stack((second,) + near[1::2]))
    )
    far = []
    for k in HOPS:
        far += [shift_z(first_y, k), shift_y(second_z, k)]
    far = lax.optimization_barrier(tuple(far))
    firsts = (first_y,) + far[0::2]
    seconds = (second_z,) + far[1::2]
    weight = jax.ShapeDtypeStruct((D, 256), BF)
    wq, wk, wv, mt = pl.pallas_call(
        fold_kernel,
        out_shape=(weight, weight, weight, jax.ShapeDtypeStruct((PDIM, 768), BF)),
        in_specs=[vmem] + [hbm] * 3,
        out_specs=(vmem,) * 4,
        scratch_shapes=[pltpu.SemaphoreType.DMA((3,))],
        compiler_params=pltpu.CompilerParams(vmem_limit_bytes=32 * 2**20),
        name="fold",
    )(patch, pinned(w_query), pinned(w_key), pinned(w_value))
    qt, block = pl.pallas_call(
        project_kernel,
        out_shape=(
            jax.ShapeDtypeStruct((NSEQ * TEXT, 256), BF),
            jax.ShapeDtypeStruct((KV_ROWS, 512), BF),
        ),
        in_specs=[smem] + [vmem] * 12,
        out_specs=(vmem,) * 2,
        scratch_shapes=[
            pltpu.VMEM((NSEQ * TEXT, D), BF),
            pltpu.VMEM((PDIM, 512), F32),
        ],
        compiler_params=pltpu.CompilerParams(vmem_limit_bytes=32 * 2**20),
        name="project",
    )(group, *firsts, *seconds, gain, wq, wk, wv)
    hops = [block] + [
        lax.ppermute(block, "seq", [(i, (i + 2 * k) % seats) for i in range(seats)])
        for k in range(1, seats // 2)
    ]
    other = [lax.ppermute(hop, "seq", [(i, i ^ 1) for i in range(seats)]) for hop in hops]
    attended, z = attend(image_seq, image_start, seat, hops, other, qt, mt, out_grad)
    parts = lax.all_to_all(z.reshape(groups * seats, 8, 128), ("dp", "seq"), 0, 0)
    grad = pl.pallas_call(
        finish_kernel,
        out_shape=jax.ShapeDtypeStruct((PDIM, PDIM), F32),
        in_specs=[vmem] * 4,
        out_specs=vmem,
        compiler_params=pltpu.CompilerParams(vmem_limit_bytes=32 * 2**20),
        name="finish",
    )(parts, lat, inv, u)
    return (attended, grad.reshape(latents.shape))


def solution(mesh):
    in_specs = (
        P(None, "seq", "dp"),
        P("dp", "seq", None),
        P(),
        P(),
        P(),
        P(),
        P(None, "dp"),
        P(None, "dp"),
        P(None, "dp"),
        P(None, "seq", "dp"),
    )
    out_specs = (P(None, "seq", "dp"), P("dp", "seq", None))
    return jax.shard_map(
        on_device, mesh=mesh, in_specs=in_specs, out_specs=out_specs, check_vma=False
    )
```

```python
import functools
import math

import jax
import jax.numpy as jnp
from jax import lax
from jax.experimental import pallas as pl
from jax.experimental.pallas import tpu as pltpu
from jax.sharding import PartitionSpec as P

HD = 128
PATCHES = 256
PDIM = 32
BLOCK = 384
TEXT = BLOCK - PATCHES
IMAGES = 16
NSEQ = 2
D = 4096
epsilon = 1e-05
SCALE = HD ** (-0.5)
LN2 = math.log(2.0)
BF = jnp.bfloat16
F32 = jnp.float32
SIDE = 4
HOPS = (1, 3, 2)
KV_ROWS = NSEQ * TEXT + 32


def dot_nn(a, b):
    return lax.dot_general(a, b, (((1,), (0,)), ((), ())), preferred_element_type=F32)


def dot_nt(a, b):
    return lax.dot_general(a, b, (((1,), (1,)), ((), ())), preferred_element_type=F32)


def own_offsets(seq_ref, start_ref, seat):
    offs = [jnp.int32(0), jnp.int32(0)]
    for i in range(IMAGES):
        rel = start_ref[i] - seat * BLOCK
        mine = (rel >= 0) & (rel < BLOCK)
        for g in range(NSEQ):
            offs[g] = jnp.where(mine & (seq_ref[i] == g), rel, offs[g])
    return offs


def pack_kernel(
    seq_hbm, start_hbm, seat_ref, text_hbm, lat_hbm, wp_hbm, gain_hbm,
    first_ref, second_ref, inv_ref, u_ref, patch_ref, gain_ref,
    seq_ref, start_ref, text_ref, lat_ref, wp_ref, sems,
):
    pairs = (
        (seq_hbm, seq_ref), (start_hbm, start_ref), (lat_hbm, lat_ref), (wp_hbm, wp_ref),
        (text_hbm, text_ref), (gain_hbm, gain_ref),
    )
    copies = [pltpu.make_async_copy(a, b, sems.at[n]) for n, (a, b) in enumerate(pairs)]
    for copy in copies:
        copy.start()
    copies[2].wait()
    copies[3].wait()
    lat = lat_ref[...]
    wp = wp_ref[...]
    embedded = dot_nn(lat, wp).astype(BF)
    emb_f = embedded.astype(F32)
    inv = lax.rsqrt(jnp.sum(emb_f * emb_f, axis=1, keepdims=True) * (1.0 / D) + epsilon)
    inv_ref[...] = jnp.broadcast_to(inv, inv_ref.shape)
    u_ref[...] = dot_nt(embedded, wp)
    scaled = lat.astype(F32) * inv
    packed = jnp.concatenate([scaled[8 * a : 8 * (a + 1)] for a in range(4)], axis=1)
    tail = jnp.concatenate([packed, jnp.zeros((8, 128), F32)], axis=0)
    tail = jnp.concatenate([tail, jnp.zeros((16, 128), F32)], axis=1).astype(BF)
    copies[0].wait()
    copies[1].wait()
    offs = own_offsets(seq_ref, start_ref, seat_ref[0])
    copies[4].wait()
    row = lax.broadcasted_iota(jnp.int32, (TEXT, 256), 0)
    for g, ref in ((0, first_ref), (1, second_ref)):
        low = text_ref[g, 0:TEXT, :].astype(F32)
        high = text_ref[g, PATCHES:BLOCK, :].astype(F32)
        ref[0:TEXT, :] = jnp.where(row < offs[g], low, high).astype(BF)
    first_ref[TEXT:, :] = tail
    copies[5].wait()
    patch_ref[...] = (wp.astype(F32) * gain_ref[...]).astype(BF)


def fold_kernel(patch_ref, wq_hbm, wk_hbm, wv_hbm, wq_ref, wk_ref, wv_ref, mt_ref, sems):
    pairs = ((wq_hbm, wq_ref), (wk_hbm, wk_ref), (wv_hbm, wv_ref))
    copies = [pltpu.make_async_copy(a, b, sems.at[n]) for n, (a, b) in enumerate(pairs)]
    for copy in copies:
        copy.start()
    for n, (_, ref) in enumerate(pairs):
        copies[n].wait()
        mt_ref[:, 256 * n : 256 * (n + 1)] = dot_nn(patch_ref[...], ref[...]).astype(BF)


def project_kernel(
    group_ref, f0, f1, f2, f3, t0, t1, t2, t3, gain_ref, wk_ref, wv_ref,
    block_ref, left, inv_ref,
    lat,
):
    rows = NSEQ * TEXT
    z_here, y_here = group_ref[0] >> 2, group_ref[0] & 3
    sums = [jnp.zeros((TEXT, 128), F32) for g in range(NSEQ)]

    def place(ref, piece, g, z, y):
        at = pl.ds(pl.multiple_of(256 * (SIDE * z + y), 256), 256)
        x = ref[piece, 0:TEXT, :].astype(F32)
        left[g * TEXT : (g + 1) * TEXT, at] = (x * gain_ref[:, at]).astype(BF)
        squares = x * x
        sums[g] = sums[g] + squares[:, :128] + squares[:, 128:]

    for n, far in enumerate((0,) + HOPS):
        for m, near in enumerate((0,) + HOPS):
            ref, z, y = (f0, f1, f2, f3)[n], (z_here - far) & 3, (y_here - near) & 3
            place(ref, m, 0, z, y)
            tile = ref[m, TEXT : TEXT + 16, 0:128].astype(F32)[0:8]
            lat[pl.ds(pl.multiple_of(8 * z, 8), 8), pl.ds(pl.multiple_of(128 * y, 128), 128)] = tile
            place((t0, t1, t2, t3)[n], m, 1, (z_here - near) & 3, (y_here - far) & 3)
    ssq = jnp.concatenate(sums, axis=0)
    inv = lax.rsqrt(jnp.sum(ssq, axis=1, keepdims=True) * (1.0 / D) + epsilon)
    block_ref[rows:, :] = lat[...].astype(BF)
    inv_ref[...] = jnp.broadcast_to(inv, inv_ref.shape)
    key = dot_nn(left[...], wk_ref[...])
    block_ref[0:rows, 0:256] = (key * inv).astype(BF)
    value = dot_nn(left[...], wv_ref[...])
    block_ref[0:rows, 256:512] = (value * inv).astype(BF)


def query_kernel(left, inv_ref, wq_ref, qt_ref):
    query = dot_nn(left[...], wq_ref[...])
    qt_ref[...] = (query * (inv_ref[:, 0:1] * (SCALE / LN2))).astype(BF)


def fold_max(s):
    return functools.reduce(jnp.maximum, [s[:, 128 * n : 128 * (n + 1)] for n in range(6)])


def fold_sum(s):
    return functools.reduce(jnp.add, [s[:, 128 * n : 128 * (n + 1)] for n in range(6)])


def position(index, offset):
    patch = 32 * ((index & 63) >> 3) + 8 * (index >> 6) + (index & 7)
    t = index - PATCHES
    return jnp.where(
        index < PATCHES, offset + patch, jnp.where(t < offset, t, t + PATCHES)
    )


def heads(h):
    return slice(h * HD, (h + 1) * HD)


def pinned(x):
    return pltpu.with_memory_space_constraint(x, pltpu.HBM)


CHAINS = [(g, h) for g in range(NSEQ) for h in range(2)]


def attend_kernel(
    seq_hbm, start_hbm, seat_ref, s0, s1, s2, s3, o0, o1, o2, o3, qt_ref, mt_ref, grad_hbm,
    out_ref, z_ref,
    labels, tiles, wide, keys, values, scores, probs, q_s, g_s, o_s, m_s, l_s, zt, zq, grad_ref, seq_ref, start_ref, sems,
):
    pairs = ((seq_hbm, seq_ref), (start_hbm, start_ref), (grad_hbm, grad_ref))
    copies = [pltpu.make_async_copy(a, b, sems.at[n]) for n, (a, b) in enumerate(pairs)]
    for copy in copies:
        copy.start()
    seat = seat_ref[0]
    chip, core = seat >> 1, seat & 1
    wide[...] = jnp.zeros_like(wide)
    for a in range(4):
        wide[128 * a + PDIM * a : 128 * a + PDIM * (a + 1), :] = mt_ref[...]
    for k in range(4):
        pair = (chip - k) & 3
        for ref, parity in (((s0, s1, s2, s3)[k], core), ((o0, o1, o2, o3)[k], 1 - core)):
            part = ref[NSEQ * TEXT :, :].astype(F32)
            at = pl.multiple_of((2 * pair + parity) * 8, 8)
            for i in range(IMAGES):
                tiles[i, pl.ds(at, 8), :] = part[
                    8 * (i // 4) : 8 * (i // 4 + 1), 128 * (i % 4) : 128 * (i % 4 + 1)
                ]
            at = pl.ds(pl.multiple_of(2 * PATCHES + TEXT * parity, TEXT), TEXT)
            for g in range(NSEQ):
                keys[g, pair, at, :] = ref[g * TEXT : (g + 1) * TEXT, 0:256]
                values[g, pair, at, :] = ref[g * TEXT : (g + 1) * TEXT, 256:512]

    copies[0].wait()
    copies[1].wait()
    offs = own_offsets(seq_ref, start_ref, seat)
    for i in range(IMAGES):
        labels[seq_ref[i] * 8 + lax.div(start_ref[i], BLOCK)] = i
    rows = lax.broadcasted_iota(jnp.int32, (BLOCK, BLOCK), 0)
    cols = lax.broadcasted_iota(jnp.int32, (BLOCK, BLOCK), 1)
    down = lax.broadcasted_iota(jnp.int32, (BLOCK, 1), 0)
    across = lax.broadcasted_iota(jnp.int32, (1, BLOCK), 1)
    for g in range(NSEQ):
        own_tile = tiles[labels[g * 8 + seat]].astype(BF)
        in_order = jnp.concatenate([tiles[labels[g * 8 + b]] for b in range(8)], axis=0).astype(BF)
        for a in range(4):
            patch = wide[128 * a : 128 * (a + 1), :]
            q_s[g, 64 * a : 64 * (a + 1), :] = (
                dot_nn(own_tile, patch[:, 0:256]) * (SCALE / LN2)
            ).astype(BF)
            kv = dot_nn(in_order, patch[:, 256:768]).astype(BF)
            for b in range(8):
                at = slice(PATCHES * (b % 2) + 64 * a, PATCHES * (b % 2) + 64 * (a + 1))
                keys[g, b // 2, at, :] = kv[64 * b : 64 * (b + 1), 0:256]
                values[g, b // 2, at, :] = kv[64 * b : 64 * (b + 1), 256:512]
        q_s[g, PATCHES:, :] = qt_ref[g * TEXT : (g + 1) * TEXT, :]
    copies[2].wait()
    for g in range(NSEQ):
        place = jnp.where(cols == position(down, offs[g]), 1.0, 0.0).astype(BF)
        g_s[g] = dot_nn(place, grad_ref[g]).astype(BF)

    def each(count, body):
        def step(p, carry):
            body(p)
            return carry

        lax.fori_loop(0, count, step, 0)

    k_col = lax.broadcasted_iota(jnp.int32, (1, 2 * BLOCK), 1)
    in_image = k_col < 2 * PATCHES
    second = jnp.where(in_image, k_col >> 8, (k_col - 2 * PATCHES) >> 7)
    k_row = jnp.where(in_image, k_col & (PATCHES - 1), PATCHES + (k_col & (TEXT - 1)))
    seen = []
    for off in offs:
        reach = jnp.where(down < PATCHES, off + (PATCHES - 1), position(down, off))
        seen.append((position(k_row, off) + BLOCK * (second - core), reach))

    def score(p, diagonal=False):
        for n, (g, h) in enumerate(CHAINS):
            s = dot_nt(q_s[g, :, heads(h)], keys[g, p, :, heads(h)])
            if diagonal:
                s = jnp.where(seen[g][0] <= seen[g][1], s, -jnp.inf)
                m_s[n] = fold_max(s)
            else:
                m_s[n] = jnp.maximum(m_s[n], fold_max(s))
            scores[n, p] = s

    score(chip, True)
    each(chip, score)

    o_s[...] = jnp.zeros_like(o_s)
    l_s[...] = jnp.zeros_like(l_s)
    for n in range(4):
        m_s[n] = jnp.broadcast_to(jnp.max(m_s[n], axis=1, keepdims=True), (BLOCK, 128))

    def weigh(p):
        for n, (g, h) in enumerate(CHAINS):
            top = m_s[n]
            lifted = jnp.exp2(scores[n, p] - jnp.concatenate([top] * 6, axis=1))
            l_s[n] += fold_sum(lifted)
            lifted = lifted.astype(BF)
            o_s[n] += dot_nn(lifted, values[g, p, :, heads(h)])
            probs[n, p] = lifted

    each(chip + 1, weigh)

    xs = []
    for g in range(NSEQ):
        outs = []
        x = []
        for h in range(2):
            n = 2 * g + h
            inv = 1.0 / jnp.sum(l_s[n], axis=1, keepdims=True)
            out = o_s[n] * inv
            outs.append(out.astype(BF))
            scaled = (g_s[g, :, heads(h)].astype(F32) * inv).astype(BF)
            delta = jnp.sum(scaled.astype(F32) * out, axis=1, keepdims=True)
            m_s[n] = jnp.broadcast_to(delta, (BLOCK, 128))
            g_s[g, :, heads(h)] = scaled
            mk = mt_ref[:, 256 + h * HD : 256 + (h + 1) * HD]
            mv = mt_ref[:, 512 + h * HD : 512 + (h + 1) * HD]
            x.append((dot_nt(mk, q_s[g, :, heads(h)]) * LN2).astype(BF))
            x.append(dot_nt(mv, scaled).astype(BF))
        xs.append(jnp.concatenate(x, axis=1))
        out_c = jnp.concatenate(outs, axis=1)
        back = jnp.where(rows == position(across, offs[g]), 1.0, 0.0).astype(BF)
        out_ref[g] = dot_nn(back, out_c).astype(BF)
    zq[...] = jnp.zeros_like(zq)
    zt[...] = jnp.zeros_like(zt)

    def differentiate(p):
        for g in range(NSEQ):
            stack = []
            for h in range(2):
                n = 2 * g + h
                delta = jnp.concatenate([m_s[n]] * 6, axis=1)
                value = values[g, p, :, heads(h)]
                dp = dot_nt(g_s[g, 0:PATCHES, heads(h)], value)
                ds = (probs[n, p, 0:PATCHES, :].astype(F32) * (dp - delta[0:PATCHES])).astype(BF)
                dp_text = dot_nt(g_s[g, PATCHES:, heads(h)], value[0 : 2 * PATCHES])
                ds_text = (
                    probs[n, p, PATCHES:, 0 : 2 * PATCHES].astype(F32)
                    * (dp_text - delta[PATCHES:, 0 : 2 * PATCHES])
                ).astype(BF)
                zq[n] += dot_nn(ds, keys[g, p, :, heads(h)])
                stack += [ds[:, 0 : 2 * PATCHES], ds_text, probs[n, p, :, 0 : 2 * PATCHES]]
            zt[g, p] = dot_nn(xs[g], jnp.concatenate(stack, axis=0))

    each(chip + 1, differentiate)

    for g in range(NSEQ):
        own = jnp.zeros((PDIM, PATCHES), F32)
        for h in range(2):
            own = own + dot_nt(mt_ref[:, heads(h)], (zq[2 * g + h] * SCALE).astype(BF))
        for b in range(8):
            flat = zt[g, b // 2, :, PATCHES * (b % 2) : PATCHES * (b % 2 + 1)]
            flat = flat + jnp.where(seat == b, own, 0.0)
            dense = jnp.concatenate([flat[:, 64 * a : 64 * (a + 1)] for a in range(4)], axis=0).T
            z_ref[labels[g * 8 + b]] = dense.astype(BF)


def attend(seq, start, seat, same, other, qt, mt, grad):
    hbm = pl.BlockSpec(memory_space=pltpu.HBM)
    smem = pl.BlockSpec(memory_space=pltpu.SMEM)
    vmem = pl.BlockSpec(memory_space=pltpu.VMEM)
    return pl.pallas_call(
        attend_kernel,
        out_shape=(
            jax.ShapeDtypeStruct((NSEQ, BLOCK, 256), BF),
            jax.ShapeDtypeStruct((IMAGES, 64, 128), BF),
        ),
        in_specs=[hbm, hbm, smem] + [vmem] * 10 + [hbm],
        out_specs=(vmem,) * 2,
        scratch_shapes=[
            pltpu.SMEM((IMAGES,), jnp.int32),
            pltpu.VMEM((IMAGES, 64, 128), F32),
            pltpu.VMEM((512, 768), BF),
            pltpu.VMEM((NSEQ, 4, 2 * BLOCK, 256), BF),
            pltpu.VMEM((NSEQ, 4, 2 * BLOCK, 256), BF),
            pltpu.VMEM((4, 4, BLOCK, 2 * BLOCK), F32),
            pltpu.VMEM((4, 4, BLOCK, 2 * BLOCK), BF),
            pltpu.VMEM((NSEQ, BLOCK, 256), BF),
            pltpu.VMEM((NSEQ, BLOCK, 256), BF),
            pltpu.VMEM((4, BLOCK, HD), F32),
            pltpu.VMEM((4, BLOCK, 128), F32),
            pltpu.VMEM((4, BLOCK, 128), F32),
            pltpu.VMEM((NSEQ, 4, PDIM, 2 * PATCHES), F32),
            pltpu.VMEM((4, PATCHES, HD), F32),
            pltpu.VMEM((NSEQ, BLOCK, 256), BF),
            pltpu.SMEM((IMAGES,), jnp.int32),
            pltpu.SMEM((IMAGES,), jnp.int32),
            pltpu.SemaphoreType.DMA((3,)),
        ],
        compiler_params=pltpu.CompilerParams(vmem_limit_bytes=44 * 2**20),
        name="attend",
    )(pinned(seq), pinned(start), seat, *same, *other, qt, mt, pinned(grad))


def finish_kernel(recv_ref, lat_ref, inv_ref, u_ref, out_ref):
    total = jnp.sum(recv_ref[...].astype(F32), axis=0)
    lat = lat_ref[...].astype(F32)
    for a in range(4):
        at = slice(8 * a, 8 * (a + 1))
        z = total[:, PDIM * a : PDIM * (a + 1)]
        inv = inv_ref[at, :][:, 0:1]
        inner = jnp.sum(lat[at] * z, axis=1, keepdims=True)
        out_ref[at, :] = inv * (z - u_ref[at, :] * (inv * inv * inner * (1.0 / D)))


def on_device(
    text_rows, latents, image_seq, image_start, norm_gain, w_patch, w_query, w_key, w_value, out_grad
):
    seats = lax.axis_size("seq")
    groups = lax.axis_size("dp")
    seat = lax.axis_index("seq").astype(jnp.int32).reshape(1)
    group = lax.axis_index("dp").astype(jnp.int32).reshape(1)
    side = SIDE
    assert groups == side * side

    def shift_y(x, k):
        pairs = [(i, i // side * side + (i + k) % side) for i in range(groups)]
        return lax.ppermute(x, "dp", pairs)

    def shift_z(x, k):
        return lax.ppermute(x, "dp", [(i, (i + side * k) % groups) for i in range(groups)])

    lat = latents.reshape(PDIM, PDIM)
    smem = pl.BlockSpec(memory_space=pltpu.SMEM)
    vmem = pl.BlockSpec(memory_space=pltpu.VMEM)
    hbm = pl.BlockSpec(memory_space=pltpu.HBM)
    first, second, inv, u, patch, gain = pl.pallas_call(
        pack_kernel,
        out_shape=(
            jax.ShapeDtypeStruct((TEXT + 16, 256), BF),
            jax.ShapeDtypeStruct((TEXT, 256), BF),
            jax.ShapeDtypeStruct((PDIM, 128), F32),
            jax.ShapeDtypeStruct((PDIM, PDIM), F32),
            jax.ShapeDtypeStruct((PDIM, D), BF),
            jax.ShapeDtypeStruct((1, D), F32),
        ),
        in_specs=[hbm, hbm, smem, hbm, hbm, hbm, hbm],
        out_specs=(vmem,) * 6,
        scratch_shapes=[
            pltpu.SMEM((IMAGES,), jnp.int32),
            pltpu.SMEM((IMAGES,), jnp.int32),
            pltpu.VMEM((NSEQ, BLOCK, 256), BF),
            pltpu.VMEM((PDIM, PDIM), BF),
            pltpu.VMEM((PDIM, D), BF),
            pltpu.SemaphoreType.DMA((6,)),
        ],
        compiler_params=pltpu.CompilerParams(vmem_limit_bytes=32 * 2**20),
        name="pack",
    )(
        pinned(image_seq), pinned(image_start), seat, pinned(text_rows), pinned(lat), pinned(w_patch),
        pinned(norm_gain.reshape(1, D)),
    )
    near = []
    for k in HOPS:
        near += [shift_y(first, k), shift_z(second, k)]
    near = lax.optimization_barrier(tuple(near))
    first_y, second_z = lax.optimization_barrier(
        (jnp.stack((first,) + near[0::2]), jnp.stack((second,) + near[1::2]))
    )
    far = []
    for k in HOPS:
        far += [shift_z(first_y, k), shift_y(second_z, k)]
    far = lax.optimization_barrier(tuple(far))
    firsts = (first_y,) + far[0::2]
    seconds = (second_z,) + far[1::2]
    weight = jax.ShapeDtypeStruct((D, 256), BF)
    wq, wk, wv, mt = pl.pallas_call(
        fold_kernel,
        out_shape=(weight, weight, weight, jax.ShapeDtypeStruct((PDIM, 768), BF)),
        in_specs=[vmem] + [hbm] * 3,
        out_specs=(vmem,) * 4,
        scratch_shapes=[pltpu.SemaphoreType.DMA((3,))],
        compiler_params=pltpu.CompilerParams(vmem_limit_bytes=32 * 2**20),
        name="fold",
    )(patch, pinned(w_query), pinned(w_key), pinned(w_value))
    block, left, text_inv = pl.pallas_call(
        project_kernel,
        out_shape=(
            jax.ShapeDtypeStruct((KV_ROWS, 512), BF),
            jax.ShapeDtypeStruct((NSEQ * TEXT, D), BF),
            jax.ShapeDtypeStruct((NSEQ * TEXT, 128), F32),
        ),
        in_specs=[smem] + [vmem] * 11,
        out_specs=(vmem,) * 3,
        scratch_shapes=[pltpu.VMEM((PDIM, 512), F32)],
        compiler_params=pltpu.CompilerParams(vmem_limit_bytes=32 * 2**20),
        name="project",
    )(group, *firsts, *seconds, gain, wk, wv)
    qt = pl.pallas_call(
        query_kernel,
        out_shape=jax.ShapeDtypeStruct((NSEQ * TEXT, 256), BF),
        in_specs=[vmem] * 3,
        out_specs=vmem,
        compiler_params=pltpu.CompilerParams(vmem_limit_bytes=32 * 2**20),
        name="query",
    )(left, text_inv, wq)
    hops = [block] + [
        lax.ppermute(block, "seq", [(i, (i + 2 * k) % seats) for i in range(seats)])
        for k in range(1, seats // 2)
    ]
    other = [lax.ppermute(hop, "seq", [(i, i ^ 1) for i in range(seats)]) for hop in hops]
    attended, z = attend(image_seq, image_start, seat, hops, other, qt, mt, out_grad)
    parts = lax.all_to_all(z.reshape(groups * seats, 8, 128), ("dp", "seq"), 0, 0)
    grad = pl.pallas_call(
        finish_kernel,
        out_shape=jax.ShapeDtypeStruct((PDIM, PDIM), F32),
        in_specs=[vmem] * 4,
        out_specs=vmem,
        compiler_params=pltpu.CompilerParams(vmem_limit_bytes=32 * 2**20),
        name="finish",
    )(parts, lat, inv, u)
    return (attended, grad.reshape(latents.shape))


def solution(mesh):
    in_specs = (
        P(None, "seq", "dp"),
        P("dp", "seq", None),
        P(),
        P(),
        P(),
        P(),
        P(None, "dp"),
        P(None, "dp"),
        P(None, "dp"),
        P(None, "seq", "dp"),
    )
    out_specs = (P(None, "seq", "dp"), P("dp", "seq", None))
    return jax.shard_map(
        on_device, mesh=mesh, in_specs=in_specs, out_specs=out_specs, check_vma=False
    )
```

```python
import functools
import math

import jax
import jax.numpy as jnp
from jax import lax
from jax.experimental import pallas as pl
from jax.experimental.pallas import tpu as pltpu
from jax.sharding import PartitionSpec as P

HD = 128
PATCHES = 256
PDIM = 32
BLOCK = 384
TEXT = BLOCK - PATCHES
IMAGES = 16
NSEQ = 2
D = 4096
epsilon = 1e-05
SCALE = HD ** (-0.5)
LN2 = math.log(2.0)
BF = jnp.bfloat16
F32 = jnp.float32
SIDE = 4
HOPS = (1, 3, 2)
KV_ROWS = NSEQ * TEXT + 32


def dot_nn(a, b):
    return lax.dot_general(a, b, (((1,), (0,)), ((), ())), preferred_element_type=F32)


def dot_nt(a, b):
    return lax.dot_general(a, b, (((1,), (1,)), ((), ())), preferred_element_type=F32)


def own_offsets(seq_ref, start_ref, seat):
    offs = [jnp.int32(0), jnp.int32(0)]
    for i in range(IMAGES):
        rel = start_ref[i] - seat * BLOCK
        mine = (rel >= 0) & (rel < BLOCK)
        for g in range(NSEQ):
            offs[g] = jnp.where(mine & (seq_ref[i] == g), rel, offs[g])
    return offs


def pack_kernel(
    seq_hbm, start_hbm, seat_ref, text_hbm, lat_hbm, wp_hbm,
    first_ref, second_ref, inv_ref, embedded_ref,
    seq_ref, start_ref, text_ref, lat_ref, wp_ref, sems,
):
    pairs = (
        (seq_hbm, seq_ref), (start_hbm, start_ref), (lat_hbm, lat_ref), (wp_hbm, wp_ref),
        (text_hbm, text_ref),
    )
    copies = [pltpu.make_async_copy(a, b, sems.at[n]) for n, (a, b) in enumerate(pairs)]
    for copy in copies:
        copy.start()
    copies[2].wait()
    copies[3].wait()
    lat = lat_ref[...]
    wp = wp_ref[...]
    embedded = dot_nn(lat, wp).astype(BF)
    emb_f = embedded.astype(F32)
    inv = lax.rsqrt(jnp.sum(emb_f * emb_f, axis=1, keepdims=True) * (1.0 / D) + epsilon)
    inv_ref[...] = jnp.broadcast_to(inv, inv_ref.shape)
    embedded_ref[...] = embedded
    scaled = lat.astype(F32) * inv
    packed = jnp.concatenate([scaled[8 * a : 8 * (a + 1)] for a in range(4)], axis=1)
    tail = jnp.concatenate([packed, jnp.zeros((8, 128), F32)], axis=0)
    tail = jnp.concatenate([tail, jnp.zeros((16, 128), F32)], axis=1).astype(BF)
    copies[0].wait()
    copies[1].wait()
    offs = own_offsets(seq_ref, start_ref, seat_ref[0])
    copies[4].wait()
    row = lax.broadcasted_iota(jnp.int32, (TEXT, 256), 0)
    for g, ref in ((0, first_ref), (1, second_ref)):
        low = text_ref[g, 0:TEXT, :].astype(F32)
        high = text_ref[g, PATCHES:BLOCK, :].astype(F32)
        ref[0:TEXT, :] = jnp.where(row < offs[g], low, high).astype(BF)
    first_ref[TEXT:, :] = tail


def fold_kernel(
    embedded_ref, wp_hbm, gain_hbm, wq_hbm, wk_hbm, wv_hbm,
    wq_ref, wk_ref, wv_ref, mt_ref, u_ref, gain_ref,
    wp_ref, sems,
):
    pairs = (
        (wp_hbm, wp_ref), (gain_hbm, gain_ref), (wq_hbm, wq_ref), (wk_hbm, wk_ref), (wv_hbm, wv_ref)
    )
    copies = [pltpu.make_async_copy(a, b, sems.at[n]) for n, (a, b) in enumerate(pairs)]
    for copy in copies:
        copy.start()
    copies[0].wait()
    copies[1].wait()
    wp = wp_ref[...]
    u_ref[...] = dot_nt(embedded_ref[...], wp)
    patch = (wp.astype(F32) * gain_ref[...]).astype(BF)
    for n, ref in enumerate((wq_ref, wk_ref, wv_ref)):
        copies[n + 2].wait()
        mt_ref[:, 256 * n : 256 * (n + 1)] = dot_nn(patch, ref[...]).astype(BF)


def project_kernel(
    group_ref, f0, f1, f2, f3, t0, t1, t2, t3, gain_ref, wk_ref, wv_ref,
    block_ref, left, inv_ref,
    lat,
):
    rows = NSEQ * TEXT
    z_here, y_here = group_ref[0] >> 2, group_ref[0] & 3
    sums = [jnp.zeros((TEXT, 128), F32) for g in range(NSEQ)]

    def place(ref, piece, g, z, y):
        at = pl.ds(pl.multiple_of(256 * (SIDE * z + y), 256), 256)
        x = ref[piece, 0:TEXT, :].astype(F32)
        left[g * TEXT : (g + 1) * TEXT, at] = (x * gain_ref[:, at]).astype(BF)
        squares = x * x
        sums[g] = sums[g] + squares[:, :128] + squares[:, 128:]

    for n, far in enumerate((0,) + HOPS):
        for m, near in enumerate((0,) + HOPS):
            ref, z, y = (f0, f1, f2, f3)[n], (z_here - far) & 3, (y_here - near) & 3
            place(ref, m, 0, z, y)
            tile = ref[m, TEXT : TEXT + 16, 0:128].astype(F32)[0:8]
            lat[pl.ds(pl.multiple_of(8 * z, 8), 8), pl.ds(pl.multiple_of(128 * y, 128), 128)] = tile
            place((t0, t1, t2, t3)[n], m, 1, (z_here - near) & 3, (y_here - far) & 3)
    ssq = jnp.concatenate(sums, axis=0)
    inv = lax.rsqrt(jnp.sum(ssq, axis=1, keepdims=True) * (1.0 / D) + epsilon)
    block_ref[rows:, :] = lat[...].astype(BF)
    inv_ref[...] = jnp.broadcast_to(inv, inv_ref.shape)
    key = dot_nn(left[...], wk_ref[...])
    block_ref[0:rows, 0:256] = (key * inv).astype(BF)
    value = dot_nn(left[...], wv_ref[...])
    block_ref[0:rows, 256:512] = (value * inv).astype(BF)


def query_kernel(left, inv_ref, wq_ref, qt_ref):
    query = dot_nn(left[...], wq_ref[...])
    qt_ref[...] = (query * (inv_ref[:, 0:1] * (SCALE / LN2))).astype(BF)


def fold_max(s):
    return functools.reduce(jnp.maximum, [s[:, 128 * n : 128 * (n + 1)] for n in range(6)])


def fold_sum(s):
    return functools.reduce(jnp.add, [s[:, 128 * n : 128 * (n + 1)] for n in range(6)])


def position(index, offset):
    patch = 32 * ((index & 63) >> 3) + 8 * (index >> 6) + (index & 7)
    t = index - PATCHES
    return jnp.where(
        index < PATCHES, offset + patch, jnp.where(t < offset, t, t + PATCHES)
    )


def heads(h):
    return slice(h * HD, (h + 1) * HD)


def pinned(x):
    return pltpu.with_memory_space_constraint(x, pltpu.HBM)


CHAINS = [(g, h) for g in range(NSEQ) for h in range(2)]


def attend_kernel(
    seq_hbm, start_hbm, seat_ref, s0, s1, s2, s3, o0, o1, o2, o3, qt_ref, mt_ref, grad_hbm,
    out_ref, z_ref,
    labels, tiles, wide, keys, values, scores, probs, q_s, g_s, o_s, m_s, l_s, zt, zq, grad_ref, seq_ref, start_ref, sems,
):
    pairs = ((seq_hbm, seq_ref), (start_hbm, start_ref), (grad_hbm, grad_ref))
    copies = [pltpu.make_async_copy(a, b, sems.at[n]) for n, (a, b) in enumerate(pairs)]
    for copy in copies:
        copy.start()
    seat = seat_ref[0]
    chip, core = seat >> 1, seat & 1
    wide[...] = jnp.zeros_like(wide)
    for a in range(4):
        wide[128 * a + PDIM * a : 128 * a + PDIM * (a + 1), :] = mt_ref[...]
    for k in range(4):
        pair = (chip - k) & 3
        for ref, parity in (((s0, s1, s2, s3)[k], core), ((o0, o1, o2, o3)[k], 1 - core)):
            part = ref[NSEQ * TEXT :, :].astype(F32)
            at = pl.multiple_of((2 * pair + parity) * 8, 8)
            for i in range(IMAGES):
                tiles[i, pl.ds(at, 8), :] = part[
                    8 * (i // 4) : 8 * (i // 4 + 1), 128 * (i % 4) : 128 * (i % 4 + 1)
                ]
            at = pl.ds(pl.multiple_of(2 * PATCHES + TEXT * parity, TEXT), TEXT)
            for g in range(NSEQ):
                keys[g, pair, at, :] = ref[g * TEXT : (g + 1) * TEXT, 0:256]
                values[g, pair, at, :] = ref[g * TEXT : (g + 1) * TEXT, 256:512]

    copies[0].wait()
    copies[1].wait()
    offs = own_offsets(seq_ref, start_ref, seat)
    for i in range(IMAGES):
        labels[seq_ref[i] * 8 + lax.div(start_ref[i], BLOCK)] = i
    rows = lax.broadcasted_iota(jnp.int32, (BLOCK, BLOCK), 0)
    cols = lax.broadcasted_iota(jnp.int32, (BLOCK, BLOCK), 1)
    down = lax.broadcasted_iota(jnp.int32, (BLOCK, 1), 0)
    across = lax.broadcasted_iota(jnp.int32, (1, BLOCK), 1)
    for g in range(NSEQ):
        own_tile = tiles[labels[g * 8 + seat]].astype(BF)
        in_order = jnp.concatenate([tiles[labels[g * 8 + b]] for b in range(8)], axis=0).astype(BF)
        for a in range(4):
            patch = wide[128 * a : 128 * (a + 1), :]
            q_s[g, 64 * a : 64 * (a + 1), :] = (
                dot_nn(own_tile, patch[:, 0:256]) * (SCALE / LN2)
            ).astype(BF)
            kv = dot_nn(in_order, patch[:, 256:768]).astype(BF)
            for b in range(8):
                at = slice(PATCHES * (b % 2) + 64 * a, PATCHES * (b % 2) + 64 * (a + 1))
                keys[g, b // 2, at, :] = kv[64 * b : 64 * (b + 1), 0:256]
                values[g, b // 2, at, :] = kv[64 * b : 64 * (b + 1), 256:512]
        q_s[g, PATCHES:, :] = qt_ref[g * TEXT : (g + 1) * TEXT, :]
    copies[2].wait()
    for g in range(NSEQ):
        place = jnp.where(cols == position(down, offs[g]), 1.0, 0.0).astype(BF)
        g_s[g] = dot_nn(place, grad_ref[g]).astype(BF)

    def each(count, body):
        def step(p, carry):
            body(p)
            return carry

        lax.fori_loop(0, count, step, 0)

    k_col = lax.broadcasted_iota(jnp.int32, (1, 2 * BLOCK), 1)
    in_image = k_col < 2 * PATCHES
    second = jnp.where(in_image, k_col >> 8, (k_col - 2 * PATCHES) >> 7)
    k_row = jnp.where(in_image, k_col & (PATCHES - 1), PATCHES + (k_col & (TEXT - 1)))
    seen = []
    for off in offs:
        reach = jnp.where(down < PATCHES, off + (PATCHES - 1), position(down, off))
        seen.append((position(k_row, off) + BLOCK * (second - core), reach))

    def score(p, diagonal=False):
        for n, (g, h) in enumerate(CHAINS):
            s = dot_nt(q_s[g, :, heads(h)], keys[g, p, :, heads(h)])
            if diagonal:
                s = jnp.where(seen[g][0] <= seen[g][1], s, -jnp.inf)
                m_s[n] = fold_max(s)
            else:
                m_s[n] = jnp.maximum(m_s[n], fold_max(s))
            scores[n, p] = s

    score(chip, True)
    each(chip, score)

    o_s[...] = jnp.zeros_like(o_s)
    l_s[...] = jnp.zeros_like(l_s)
    for n in range(4):
        m_s[n] = jnp.broadcast_to(jnp.max(m_s[n], axis=1, keepdims=True), (BLOCK, 128))

    def weigh(p):
        for n, (g, h) in enumerate(CHAINS):
            top = m_s[n]
            lifted = jnp.exp2(scores[n, p] - jnp.concatenate([top] * 6, axis=1))
            l_s[n] += fold_sum(lifted)
            lifted = lifted.astype(BF)
            o_s[n] += dot_nn(lifted, values[g, p, :, heads(h)])
            probs[n, p] = lifted

    each(chip + 1, weigh)

    xs = []
    for g in range(NSEQ):
        outs = []
        x = []
        for h in range(2):
            n = 2 * g + h
            inv = 1.0 / jnp.sum(l_s[n], axis=1, keepdims=True)
            out = o_s[n] * inv
            outs.append(out.astype(BF))
            scaled = (g_s[g, :, heads(h)].astype(F32) * inv).astype(BF)
            delta = jnp.sum(scaled.astype(F32) * out, axis=1, keepdims=True)
            m_s[n] = jnp.broadcast_to(delta, (BLOCK, 128))
            g_s[g, :, heads(h)] = scaled
            mk = mt_ref[:, 256 + h * HD : 256 + (h + 1) * HD]
            mv = mt_ref[:, 512 + h * HD : 512 + (h + 1) * HD]
            x.append((dot_nt(mk, q_s[g, :, heads(h)]) * LN2).astype(BF))
            x.append(dot_nt(mv, scaled).astype(BF))
        xs.append(jnp.concatenate(x, axis=1))
        out_c = jnp.concatenate(outs, axis=1)
        back = jnp.where(rows == position(across, offs[g]), 1.0, 0.0).astype(BF)
        out_ref[g] = dot_nn(back, out_c).astype(BF)
    zq[...] = jnp.zeros_like(zq)
    zt[...] = jnp.zeros_like(zt)

    def differentiate(p):
        for g in range(NSEQ):
            stack = []
            for h in range(2):
                n = 2 * g + h
                delta = jnp.concatenate([m_s[n]] * 6, axis=1)
                value = values[g, p, :, heads(h)]
                dp = dot_nt(g_s[g, 0:PATCHES, heads(h)], value)
                ds = (probs[n, p, 0:PATCHES, :].astype(F32) * (dp - delta[0:PATCHES])).astype(BF)
                dp_text = dot_nt(g_s[g, PATCHES:, heads(h)], value[0 : 2 * PATCHES])
                ds_text = (
                    probs[n, p, PATCHES:, 0 : 2 * PATCHES].astype(F32)
                    * (dp_text - delta[PATCHES:, 0 : 2 * PATCHES])
                ).astype(BF)
                zq[n] += dot_nn(ds, keys[g, p, :, heads(h)])
                stack += [ds[:, 0 : 2 * PATCHES], ds_text, probs[n, p, :, 0 : 2 * PATCHES]]
            zt[g, p] = dot_nn(xs[g], jnp.concatenate(stack, axis=0))

    each(chip + 1, differentiate)

    for g in range(NSEQ):
        own = jnp.zeros((PDIM, PATCHES), F32)
        for h in range(2):
            own = own + dot_nt(mt_ref[:, heads(h)], (zq[2 * g + h] * SCALE).astype(BF))
        for b in range(8):
            flat = zt[g, b // 2, :, PATCHES * (b % 2) : PATCHES * (b % 2 + 1)]
            flat = flat + jnp.where(seat == b, own, 0.0)
            dense = jnp.concatenate([flat[:, 64 * a : 64 * (a + 1)] for a in range(4)], axis=0).T
            z_ref[labels[g * 8 + b]] = dense.astype(BF)


def attend(seq, start, seat, same, other, qt, mt, grad):
    hbm = pl.BlockSpec(memory_space=pltpu.HBM)
    smem = pl.BlockSpec(memory_space=pltpu.SMEM)
    vmem = pl.BlockSpec(memory_space=pltpu.VMEM)
    return pl.pallas_call(
        attend_kernel,
        out_shape=(
            jax.ShapeDtypeStruct((NSEQ, BLOCK, 256), BF),
            jax.ShapeDtypeStruct((IMAGES, 64, 128), BF),
        ),
        in_specs=[hbm, hbm, smem] + [vmem] * 10 + [hbm],
        out_specs=(vmem,) * 2,
        scratch_shapes=[
            pltpu.SMEM((IMAGES,), jnp.int32),
            pltpu.VMEM((IMAGES, 64, 128), F32),
            pltpu.VMEM((512, 768), BF),
            pltpu.VMEM((NSEQ, 4, 2 * BLOCK, 256), BF),
            pltpu.VMEM((NSEQ, 4, 2 * BLOCK, 256), BF),
            pltpu.VMEM((4, 4, BLOCK, 2 * BLOCK), F32),
            pltpu.VMEM((4, 4, BLOCK, 2 * BLOCK), BF),
            pltpu.VMEM((NSEQ, BLOCK, 256), BF),
            pltpu.VMEM((NSEQ, BLOCK, 256), BF),
            pltpu.VMEM((4, BLOCK, HD), F32),
            pltpu.VMEM((4, BLOCK, 128), F32),
            pltpu.VMEM((4, BLOCK, 128), F32),
            pltpu.VMEM((NSEQ, 4, PDIM, 2 * PATCHES), F32),
            pltpu.VMEM((4, PATCHES, HD), F32),
            pltpu.VMEM((NSEQ, BLOCK, 256), BF),
            pltpu.SMEM((IMAGES,), jnp.int32),
            pltpu.SMEM((IMAGES,), jnp.int32),
            pltpu.SemaphoreType.DMA((3,)),
        ],
        compiler_params=pltpu.CompilerParams(vmem_limit_bytes=44 * 2**20),
        name="attend",
    )(pinned(seq), pinned(start), seat, *same, *other, qt, mt, pinned(grad))


def finish_kernel(recv_ref, lat_ref, inv_ref, u_ref, out_ref):
    total = jnp.sum(recv_ref[...].astype(F32), axis=0)
    lat = lat_ref[...].astype(F32)
    for a in range(4):
        at = slice(8 * a, 8 * (a + 1))
        z = total[:, PDIM * a : PDIM * (a + 1)]
        inv = inv_ref[at, :][:, 0:1]
        inner = jnp.sum(lat[at] * z, axis=1, keepdims=True)
        out_ref[at, :] = inv * (z - u_ref[at, :] * (inv * inv * inner * (1.0 / D)))


def on_device(
    text_rows, latents, image_seq, image_start, norm_gain, w_patch, w_query, w_key, w_value, out_grad
):
    seats = lax.axis_size("seq")
    groups = lax.axis_size("dp")
    seat = lax.axis_index("seq").astype(jnp.int32).reshape(1)
    group = lax.axis_index("dp").astype(jnp.int32).reshape(1)
    side = SIDE
    assert groups == side * side

    def shift_y(x, k):
        pairs = [(i, i // side * side + (i + k) % side) for i in range(groups)]
        return lax.ppermute(x, "dp", pairs)

    def shift_z(x, k):
        return lax.ppermute(x, "dp", [(i, (i + side * k) % groups) for i in range(groups)])

    lat = latents.reshape(PDIM, PDIM)
    smem = pl.BlockSpec(memory_space=pltpu.SMEM)
    vmem = pl.BlockSpec(memory_space=pltpu.VMEM)
    hbm = pl.BlockSpec(memory_space=pltpu.HBM)
    first, second, inv, embedded = pl.pallas_call(
        pack_kernel,
        out_shape=(
            jax.ShapeDtypeStruct((TEXT + 16, 256), BF),
            jax.ShapeDtypeStruct((TEXT, 256), BF),
            jax.ShapeDtypeStruct((PDIM, 128), F32),
            jax.ShapeDtypeStruct((PDIM, D), BF),
        ),
        in_specs=[hbm, hbm, smem, hbm, hbm, hbm],
        out_specs=(vmem,) * 4,
        scratch_shapes=[
            pltpu.SMEM((IMAGES,), jnp.int32),
            pltpu.SMEM((IMAGES,), jnp.int32),
            pltpu.VMEM((NSEQ, BLOCK, 256), BF),
            pltpu.VMEM((PDIM, PDIM), BF),
            pltpu.VMEM((PDIM, D), BF),
            pltpu.SemaphoreType.DMA((5,)),
        ],
        compiler_params=pltpu.CompilerParams(vmem_limit_bytes=32 * 2**20),
        name="pack",
    )(
        pinned(image_seq), pinned(image_start), seat, pinned(text_rows), pinned(lat), pinned(w_patch),
    )
    near = []
    for k in HOPS:
        near += [shift_y(first, k), shift_z(second, k)]
    near = lax.optimization_barrier(tuple(near))
    first_y, second_z = lax.optimization_barrier(
        (jnp.stack((first,) + near[0::2]), jnp.stack((second,) + near[1::2]))
    )
    far = []
    for k in HOPS:
        far += [shift_z(first_y, k), shift_y(second_z, k)]
    far = lax.optimization_barrier(tuple(far))
    firsts = (first_y,) + far[0::2]
    seconds = (second_z,) + far[1::2]
    weight = jax.ShapeDtypeStruct((D, 256), BF)
    wq, wk, wv, mt, u, gain = pl.pallas_call(
        fold_kernel,
        out_shape=(
            weight,
            weight,
            weight,
            jax.ShapeDtypeStruct((PDIM, 768), BF),
            jax.ShapeDtypeStruct((PDIM, PDIM), F32),
            jax.ShapeDtypeStruct((1, D), F32),
        ),
        in_specs=[vmem] + [hbm] * 5,
        out_specs=(vmem,) * 6,
        scratch_shapes=[pltpu.VMEM((PDIM, D), BF), pltpu.SemaphoreType.DMA((5,))],
        compiler_params=pltpu.CompilerParams(vmem_limit_bytes=32 * 2**20),
        name="fold",
    )(
        embedded, pinned(w_patch), pinned(norm_gain.reshape(1, D)),
        pinned(w_query), pinned(w_key), pinned(w_value),
    )
    block, left, text_inv = pl.pallas_call(
        project_kernel,
        out_shape=(
            jax.ShapeDtypeStruct((KV_ROWS, 512), BF),
            jax.ShapeDtypeStruct((NSEQ * TEXT, D), BF),
            jax.ShapeDtypeStruct((NSEQ * TEXT, 128), F32),
        ),
        in_specs=[smem] + [vmem] * 11,
        out_specs=(vmem,) * 3,
        scratch_shapes=[pltpu.VMEM((PDIM, 512), F32)],
        compiler_params=pltpu.CompilerParams(vmem_limit_bytes=32 * 2**20),
        name="project",
    )(group, *firsts, *seconds, gain, wk, wv)
    qt = pl.pallas_call(
        query_kernel,
        out_shape=jax.ShapeDtypeStruct((NSEQ * TEXT, 256), BF),
        in_specs=[vmem] * 3,
        out_specs=vmem,
        compiler_params=pltpu.CompilerParams(vmem_limit_bytes=32 * 2**20),
        name="query",
    )(left, text_inv, wq)
    hops = [block] + [
        lax.ppermute(block, "seq", [(i, (i + 2 * k) % seats) for i in range(seats)])
        for k in range(1, seats // 2)
    ]
    other = [lax.ppermute(hop, "seq", [(i, i ^ 1) for i in range(seats)]) for hop in hops]
    attended, z = attend(image_seq, image_start, seat, hops, other, qt, mt, out_grad)
    parts = lax.all_to_all(z.reshape(groups * seats, 8, 128), ("dp", "seq"), 0, 0)
    grad = pl.pallas_call(
        finish_kernel,
        out_shape=jax.ShapeDtypeStruct((PDIM, PDIM), F32),
        in_specs=[vmem] * 4,
        out_specs=vmem,
        compiler_params=pltpu.CompilerParams(vmem_limit_bytes=32 * 2**20),
        name="finish",
    )(parts, lat, inv, u)
    return (attended, grad.reshape(latents.shape))


def solution(mesh):
    in_specs = (
        P(None, "seq", "dp"),
        P("dp", "seq", None),
        P(),
        P(),
        P(),
        P(),
        P(None, "dp"),
        P(None, "dp"),
        P(None, "dp"),
        P(None, "seq", "dp"),
    )
    out_specs = (P(None, "seq", "dp"), P("dp", "seq", None))
    return jax.shard_map(
        on_device, mesh=mesh, in_specs=in_specs, out_specs=out_specs, check_vma=False
    )
```

```python
import functools
import math

import jax
import jax.numpy as jnp
from jax import lax
from jax.experimental import pallas as pl
from jax.experimental.pallas import tpu as pltpu
from jax.sharding import PartitionSpec as P

HD = 128
PATCHES = 256
PDIM = 32
BLOCK = 384
TEXT = BLOCK - PATCHES
IMAGES = 16
NSEQ = 2
D = 4096
epsilon = 1e-05
SCALE = HD ** (-0.5)
LN2 = math.log(2.0)
BF = jnp.bfloat16
F32 = jnp.float32
SIDE = 4
HOPS = (1, 3, 2)
KV_ROWS = NSEQ * TEXT + 32


def dot_nn(a, b):
    return lax.dot_general(a, b, (((1,), (0,)), ((), ())), preferred_element_type=F32)


def dot_nt(a, b):
    return lax.dot_general(a, b, (((1,), (1,)), ((), ())), preferred_element_type=F32)


def own_offsets(seq_ref, start_ref, seat):
    offs = [jnp.int32(0), jnp.int32(0)]
    for i in range(IMAGES):
        rel = start_ref[i] - seat * BLOCK
        mine = (rel >= 0) & (rel < BLOCK)
        for g in range(NSEQ):
            offs[g] = jnp.where(mine & (seq_ref[i] == g), rel, offs[g])
    return offs


def pack_kernel(
    seq_hbm, start_hbm, seat_ref, text_hbm, lat_hbm, wp_hbm,
    first_ref, second_ref, inv_ref, embedded_ref,
    seq_ref, start_ref, text_ref, lat_ref, wp_ref, sems,
):
    pairs = (
        (seq_hbm, seq_ref), (start_hbm, start_ref), (lat_hbm, lat_ref), (wp_hbm, wp_ref),
        (text_hbm, text_ref),
    )
    copies = [pltpu.make_async_copy(a, b, sems.at[n]) for n, (a, b) in enumerate(pairs)]
    for copy in copies:
        copy.start()
    copies[2].wait()
    copies[3].wait()
    lat = lat_ref[...]
    wp = wp_ref[...]
    embedded = dot_nn(lat, wp).astype(BF)
    emb_f = embedded.astype(F32)
    inv = lax.rsqrt(jnp.sum(emb_f * emb_f, axis=1, keepdims=True) * (1.0 / D) + epsilon)
    inv_ref[...] = jnp.broadcast_to(inv, inv_ref.shape)
    embedded_ref[...] = embedded
    scaled = lat.astype(F32) * inv
    packed = jnp.concatenate([scaled[8 * a : 8 * (a + 1)] for a in range(4)], axis=1)
    tail = jnp.concatenate([packed, jnp.zeros((8, 128), F32)], axis=0)
    tail = jnp.concatenate([tail, jnp.zeros((16, 128), F32)], axis=1).astype(BF)
    copies[0].wait()
    copies[1].wait()
    offs = own_offsets(seq_ref, start_ref, seat_ref[0])
    copies[4].wait()
    row = lax.broadcasted_iota(jnp.int32, (TEXT, 256), 0)
    for g, ref in ((0, first_ref), (1, second_ref)):
        low = text_ref[g, 0:TEXT, :].astype(F32)
        high = text_ref[g, PATCHES:BLOCK, :].astype(F32)
        ref[0:TEXT, :] = jnp.where(row < offs[g], low, high).astype(BF)
    first_ref[TEXT:, :] = tail


def fold_kernel(
    embedded_ref, wp_hbm, gain_hbm, wq_hbm, wk_hbm, wv_hbm,
    wq_ref, wk_ref, wv_ref, mt_ref, u_ref, gain_ref,
    wp_ref, sems,
):
    pairs = (
        (wp_hbm, wp_ref), (gain_hbm, gain_ref), (wq_hbm, wq_ref), (wk_hbm, wk_ref), (wv_hbm, wv_ref)
    )
    copies = [pltpu.make_async_copy(a, b, sems.at[n]) for n, (a, b) in enumerate(pairs)]
    for copy in copies:
        copy.start()
    copies[0].wait()
    copies[1].wait()
    wp = wp_ref[...]
    u_ref[...] = dot_nt(embedded_ref[...], wp)
    patch = (wp.astype(F32) * gain_ref[...]).astype(BF)
    for n, ref in enumerate((wq_ref, wk_ref, wv_ref)):
        copies[n + 2].wait()
        mt_ref[:, 256 * n : 256 * (n + 1)] = dot_nn(patch, ref[...]).astype(BF)


def project_kernel(
    group_ref, f0, f1, f2, f3, t0, t1, t2, t3, gain_ref, wk_ref, wv_ref,
    block_ref, left, inv_ref,
    lat,
):
    rows = NSEQ * TEXT
    z_here, y_here = group_ref[0] >> 2, group_ref[0] & 3
    sums = [jnp.zeros((TEXT, 128), F32) for g in range(NSEQ)]

    def place(ref, piece, g, z, y):
        at = pl.ds(pl.multiple_of(256 * (SIDE * z + y), 256), 256)
        x = ref[piece, 0:TEXT, :].astype(F32)
        left[g * TEXT : (g + 1) * TEXT, at] = (x * gain_ref[:, at]).astype(BF)
        squares = x * x
        sums[g] = sums[g] + squares[:, :128] + squares[:, 128:]

    for n, far in enumerate((0,) + HOPS):
        for m, near in enumerate((0,) + HOPS):
            ref, z, y = (f0, f1, f2, f3)[n], (z_here - far) & 3, (y_here - near) & 3
            place(ref, m, 0, z, y)
            tile = ref[m, TEXT : TEXT + 16, 0:128].astype(F32)[0:8]
            lat[pl.ds(pl.multiple_of(8 * z, 8), 8), pl.ds(pl.multiple_of(128 * y, 128), 128)] = tile
            place((t0, t1, t2, t3)[n], m, 1, (z_here - near) & 3, (y_here - far) & 3)
    ssq = jnp.concatenate(sums, axis=0)
    inv = lax.rsqrt(jnp.sum(ssq, axis=1, keepdims=True) * (1.0 / D) + epsilon)
    block_ref[rows:, :] = lat[...].astype(BF)
    inv_ref[...] = jnp.broadcast_to(inv, inv_ref.shape)
    key = dot_nn(left[...], wk_ref[...])
    block_ref[0:rows, 0:256] = (key * inv).astype(BF)
    value = dot_nn(left[...], wv_ref[...])
    block_ref[0:rows, 256:512] = (value * inv).astype(BF)


def query_kernel(left, inv_ref, wq_ref, qt_ref):
    query = dot_nn(left[...], wq_ref[...])
    qt_ref[...] = (query * (inv_ref[:, 0:1] * (SCALE / LN2))).astype(BF)


def fold_max(s):
    return functools.reduce(jnp.maximum, [s[:, 128 * n : 128 * (n + 1)] for n in range(6)])


def fold_sum(s):
    return functools.reduce(jnp.add, [s[:, 128 * n : 128 * (n + 1)] for n in range(6)])


def position(index, offset):
    patch = 32 * ((index & 63) >> 3) + 8 * (index >> 6) + (index & 7)
    t = index - PATCHES
    return jnp.where(
        index < PATCHES, offset + patch, jnp.where(t < offset, t, t + PATCHES)
    )


def heads(h):
    return slice(h * HD, (h + 1) * HD)


def pinned(x):
    return pltpu.with_memory_space_constraint(x, pltpu.HBM)


CHAINS = [(g, h) for g in range(NSEQ) for h in range(2)]


def attend_kernel(
    seq_hbm, start_hbm, seat_ref, s0, s1, s2, s3, o0, o1, o2, o3, qt_ref, mt_ref, grad_hbm,
    out_ref, z_ref,
    labels, tiles, wide, keys, values, scores, probs, q_s, g_s, o_s, m_s, l_s, zt, zq, grad_ref, seq_ref, start_ref, sems,
):
    pairs = ((seq_hbm, seq_ref), (start_hbm, start_ref), (grad_hbm, grad_ref))
    copies = [pltpu.make_async_copy(a, b, sems.at[n]) for n, (a, b) in enumerate(pairs)]
    for copy in copies:
        copy.start()
    seat = seat_ref[0]
    chip, core = seat >> 1, seat & 1
    wide[...] = jnp.zeros_like(wide)
    for a in range(4):
        wide[128 * a + PDIM * a : 128 * a + PDIM * (a + 1), :] = mt_ref[...]
    for k in range(4):
        pair = (chip - k) & 3
        for ref, parity in (((s0, s1, s2, s3)[k], core), ((o0, o1, o2, o3)[k], 1 - core)):
            part = ref[NSEQ * TEXT :, :].astype(F32)
            at = pl.multiple_of((2 * pair + parity) * 8, 8)
            for i in range(IMAGES):
                tiles[i, pl.ds(at, 8), :] = part[
                    8 * (i // 4) : 8 * (i // 4 + 1), 128 * (i % 4) : 128 * (i % 4 + 1)
                ]
            at = pl.ds(pl.multiple_of(2 * PATCHES + TEXT * parity, TEXT), TEXT)
            for g in range(NSEQ):
                keys[g, pair, at, :] = ref[g * TEXT : (g + 1) * TEXT, 0:256]
                values[g, pair, at, :] = ref[g * TEXT : (g + 1) * TEXT, 256:512]

    copies[0].wait()
    copies[1].wait()
    offs = own_offsets(seq_ref, start_ref, seat)
    for i in range(IMAGES):
        labels[seq_ref[i] * 8 + lax.div(start_ref[i], BLOCK)] = i
    rows = lax.broadcasted_iota(jnp.int32, (BLOCK, BLOCK), 0)
    cols = lax.broadcasted_iota(jnp.int32, (BLOCK, BLOCK), 1)
    down = lax.broadcasted_iota(jnp.int32, (BLOCK, 1), 0)
    across = lax.broadcasted_iota(jnp.int32, (1, BLOCK), 1)
    for g in range(NSEQ):
        own_tile = tiles[labels[g * 8 + seat]].astype(BF)
        in_order = jnp.concatenate([tiles[labels[g * 8 + b]] for b in range(8)], axis=0).astype(BF)
        for a in range(4):
            patch = wide[128 * a : 128 * (a + 1), :]
            q_s[g, 64 * a : 64 * (a + 1), :] = (
                dot_nn(own_tile, patch[:, 0:256]) * (SCALE / LN2)
            ).astype(BF)
            kv = dot_nn(in_order, patch[:, 256:768]).astype(BF)
            for b in range(8):
                at = slice(PATCHES * (b % 2) + 64 * a, PATCHES * (b % 2) + 64 * (a + 1))
                keys[g, b // 2, at, :] = kv[64 * b : 64 * (b + 1), 0:256]
                values[g, b // 2, at, :] = kv[64 * b : 64 * (b + 1), 256:512]
        q_s[g, PATCHES:, :] = qt_ref[g * TEXT : (g + 1) * TEXT, :]
    copies[2].wait()
    for g in range(NSEQ):
        place = jnp.where(cols == position(down, offs[g]), 1.0, 0.0).astype(BF)
        g_s[g] = dot_nn(place, grad_ref[g]).astype(BF)

    def each(count, body, most):
        def step(p, carry):
            body(p)
            return carry

        def flat():
            for p in range(most):
                body(p)

        pl.when(count == most)(flat)
        def rolled():
            lax.fori_loop(0, count, step, 0)

        pl.when(count < most)(rolled)

    k_col = lax.broadcasted_iota(jnp.int32, (1, 2 * BLOCK), 1)
    in_image = k_col < 2 * PATCHES
    second = jnp.where(in_image, k_col >> 8, (k_col - 2 * PATCHES) >> 7)
    k_row = jnp.where(in_image, k_col & (PATCHES - 1), PATCHES + (k_col & (TEXT - 1)))
    seen = []
    for off in offs:
        reach = jnp.where(down < PATCHES, off + (PATCHES - 1), position(down, off))
        seen.append((position(k_row, off) + BLOCK * (second - core), reach))

    def score(p, diagonal=False):
        for n, (g, h) in enumerate(CHAINS):
            s = dot_nt(q_s[g, :, heads(h)], keys[g, p, :, heads(h)])
            if diagonal:
                s = jnp.where(seen[g][0] <= seen[g][1], s, -jnp.inf)
                m_s[n] = fold_max(s)
            else:
                m_s[n] = jnp.maximum(m_s[n], fold_max(s))
            scores[n, p] = s

    score(chip, True)
    each(chip, score, 3)

    o_s[...] = jnp.zeros_like(o_s)
    l_s[...] = jnp.zeros_like(l_s)
    for n in range(4):
        m_s[n] = jnp.broadcast_to(jnp.max(m_s[n], axis=1, keepdims=True), (BLOCK, 128))

    def weigh(p):
        for n, (g, h) in enumerate(CHAINS):
            top = m_s[n]
            lifted = jnp.exp2(scores[n, p] - jnp.concatenate([top] * 6, axis=1))
            l_s[n] += fold_sum(lifted)
            lifted = lifted.astype(BF)
            o_s[n] += dot_nn(lifted, values[g, p, :, heads(h)])
            probs[n, p] = lifted

    each(chip + 1, weigh, 4)

    xs = []
    for g in range(NSEQ):
        outs = []
        x = []
        for h in range(2):
            n = 2 * g + h
            inv = 1.0 / jnp.sum(l_s[n], axis=1, keepdims=True)
            out = o_s[n] * inv
            outs.append(out.astype(BF))
            scaled = (g_s[g, :, heads(h)].astype(F32) * inv).astype(BF)
            delta = jnp.sum(scaled.astype(F32) * out, axis=1, keepdims=True)
            m_s[n] = jnp.broadcast_to(delta, (BLOCK, 128))
            g_s[g, :, heads(h)] = scaled
            mk = mt_ref[:, 256 + h * HD : 256 + (h + 1) * HD]
            mv = mt_ref[:, 512 + h * HD : 512 + (h + 1) * HD]
            x.append((dot_nt(mk, q_s[g, :, heads(h)]) * LN2).astype(BF))
            x.append(dot_nt(mv, scaled).astype(BF))
        xs.append(jnp.concatenate(x, axis=1))
        out_c = jnp.concatenate(outs, axis=1)
        back = jnp.where(rows == position(across, offs[g]), 1.0, 0.0).astype(BF)
        out_ref[g] = dot_nn(back, out_c).astype(BF)
    zq[...] = jnp.zeros_like(zq)
    zt[...] = jnp.zeros_like(zt)

    def differentiate(p):
        for g in range(NSEQ):
            stack = []
            for h in range(2):
                n = 2 * g + h
                delta = jnp.concatenate([m_s[n]] * 6, axis=1)
                value = values[g, p, :, heads(h)]
                dp = dot_nt(g_s[g, 0:PATCHES, heads(h)], value)
                ds = (probs[n, p, 0:PATCHES, :].astype(F32) * (dp - delta[0:PATCHES])).astype(BF)
                dp_text = dot_nt(g_s[g, PATCHES:, heads(h)], value[0 : 2 * PATCHES])
                ds_text = (
                    probs[n, p, PATCHES:, 0 : 2 * PATCHES].astype(F32)
                    * (dp_text - delta[PATCHES:, 0 : 2 * PATCHES])
                ).astype(BF)
                zq[n] += dot_nn(ds, keys[g, p, :, heads(h)])
                stack += [ds[:, 0 : 2 * PATCHES], ds_text, probs[n, p, :, 0 : 2 * PATCHES]]
            zt[g, p] = dot_nn(xs[g], jnp.concatenate(stack, axis=0))

    each(chip + 1, differentiate, 4)

    for g in range(NSEQ):
        own = jnp.zeros((PDIM, PATCHES), F32)
        for h in range(2):
            own = own + dot_nt(mt_ref[:, heads(h)], (zq[2 * g + h] * SCALE).astype(BF))
        for b in range(8):
            flat = zt[g, b // 2, :, PATCHES * (b % 2) : PATCHES * (b % 2 + 1)]
            flat = flat + jnp.where(seat == b, own, 0.0)
            dense = jnp.concatenate([flat[:, 64 * a : 64 * (a + 1)] for a in range(4)], axis=0).T
            z_ref[labels[g * 8 + b]] = dense.astype(BF)


def attend(seq, start, seat, same, other, qt, mt, grad):
    hbm = pl.BlockSpec(memory_space=pltpu.HBM)
    smem = pl.BlockSpec(memory_space=pltpu.SMEM)
    vmem = pl.BlockSpec(memory_space=pltpu.VMEM)
    return pl.pallas_call(
        attend_kernel,
        out_shape=(
            jax.ShapeDtypeStruct((NSEQ, BLOCK, 256), BF),
            jax.ShapeDtypeStruct((IMAGES, 64, 128), BF),
        ),
        in_specs=[hbm, hbm, smem] + [vmem] * 10 + [hbm],
        out_specs=(vmem,) * 2,
        scratch_shapes=[
            pltpu.SMEM((IMAGES,), jnp.int32),
            pltpu.VMEM((IMAGES, 64, 128), F32),
            pltpu.VMEM((512, 768), BF),
            pltpu.VMEM((NSEQ, 4, 2 * BLOCK, 256), BF),
            pltpu.VMEM((NSEQ, 4, 2 * BLOCK, 256), BF),
            pltpu.VMEM((4, 4, BLOCK, 2 * BLOCK), F32),
            pltpu.VMEM((4, 4, BLOCK, 2 * BLOCK), BF),
            pltpu.VMEM((NSEQ, BLOCK, 256), BF),
            pltpu.VMEM((NSEQ, BLOCK, 256), BF),
            pltpu.VMEM((4, BLOCK, HD), F32),
            pltpu.VMEM((4, BLOCK, 128), F32),
            pltpu.VMEM((4, BLOCK, 128), F32),
            pltpu.VMEM((NSEQ, 4, PDIM, 2 * PATCHES), F32),
            pltpu.VMEM((4, PATCHES, HD), F32),
            pltpu.VMEM((NSEQ, BLOCK, 256), BF),
            pltpu.SMEM((IMAGES,), jnp.int32),
            pltpu.SMEM((IMAGES,), jnp.int32),
            pltpu.SemaphoreType.DMA((3,)),
        ],
        compiler_params=pltpu.CompilerParams(vmem_limit_bytes=44 * 2**20),
        name="attend",
    )(pinned(seq), pinned(start), seat, *same, *other, qt, mt, pinned(grad))


def finish_kernel(recv_ref, lat_ref, inv_ref, u_ref, out_ref):
    total = jnp.sum(recv_ref[...].astype(F32), axis=0)
    lat = lat_ref[...].astype(F32)
    for a in range(4):
        at = slice(8 * a, 8 * (a + 1))
        z = total[:, PDIM * a : PDIM * (a + 1)]
        inv = inv_ref[at, :][:, 0:1]
        inner = jnp.sum(lat[at] * z, axis=1, keepdims=True)
        out_ref[at, :] = inv * (z - u_ref[at, :] * (inv * inv * inner * (1.0 / D)))


def on_device(
    text_rows, latents, image_seq, image_start, norm_gain, w_patch, w_query, w_key, w_value, out_grad
):
    seats = lax.axis_size("seq")
    groups = lax.axis_size("dp")
    seat = lax.axis_index("seq").astype(jnp.int32).reshape(1)
    group = lax.axis_index("dp").astype(jnp.int32).reshape(1)
    side = SIDE
    assert groups == side * side

    def shift_y(x, k):
        pairs = [(i, i // side * side + (i + k) % side) for i in range(groups)]
        return lax.ppermute(x, "dp", pairs)

    def shift_z(x, k):
        return lax.ppermute(x, "dp", [(i, (i + side * k) % groups) for i in range(groups)])

    lat = latents.reshape(PDIM, PDIM)
    smem = pl.BlockSpec(memory_space=pltpu.SMEM)
    vmem = pl.BlockSpec(memory_space=pltpu.VMEM)
    hbm = pl.BlockSpec(memory_space=pltpu.HBM)
    first, second, inv, embedded = pl.pallas_call(
        pack_kernel,
        out_shape=(
            jax.ShapeDtypeStruct((TEXT + 16, 256), BF),
            jax.ShapeDtypeStruct((TEXT, 256), BF),
            jax.ShapeDtypeStruct((PDIM, 128), F32),
            jax.ShapeDtypeStruct((PDIM, D), BF),
        ),
        in_specs=[hbm, hbm, smem, hbm, hbm, hbm],
        out_specs=(vmem,) * 4,
        scratch_shapes=[
            pltpu.SMEM((IMAGES,), jnp.int32),
            pltpu.SMEM((IMAGES,), jnp.int32),
            pltpu.VMEM((NSEQ, BLOCK, 256), BF),
            pltpu.VMEM((PDIM, PDIM), BF),
            pltpu.VMEM((PDIM, D), BF),
            pltpu.SemaphoreType.DMA((5,)),
        ],
        compiler_params=pltpu.CompilerParams(vmem_limit_bytes=32 * 2**20),
        name="pack",
    )(
        pinned(image_seq), pinned(image_start), seat, pinned(text_rows), pinned(lat), pinned(w_patch),
    )
    near = []
    for k in HOPS:
        near += [shift_y(first, k), shift_z(second, k)]
    near = lax.optimization_barrier(tuple(near))
    first_y, second_z = lax.optimization_barrier(
        (jnp.stack((first,) + near[0::2]), jnp.stack((second,) + near[1::2]))
    )
    far = []
    for k in HOPS:
        far += [shift_z(first_y, k), shift_y(second_z, k)]
    far = lax.optimization_barrier(tuple(far))
    firsts = (first_y,) + far[0::2]
    seconds = (second_z,) + far[1::2]
    weight = jax.ShapeDtypeStruct((D, 256), BF)
    wq, wk, wv, mt, u, gain = pl.pallas_call(
        fold_kernel,
        out_shape=(
            weight,
            weight,
            weight,
            jax.ShapeDtypeStruct((PDIM, 768), BF),
            jax.ShapeDtypeStruct((PDIM, PDIM), F32),
            jax.ShapeDtypeStruct((1, D), F32),
        ),
        in_specs=[vmem] + [hbm] * 5,
        out_specs=(vmem,) * 6,
        scratch_shapes=[pltpu.VMEM((PDIM, D), BF), pltpu.SemaphoreType.DMA((5,))],
        compiler_params=pltpu.CompilerParams(vmem_limit_bytes=32 * 2**20),
        name="fold",
    )(
        embedded, pinned(w_patch), pinned(norm_gain.reshape(1, D)),
        pinned(w_query), pinned(w_key), pinned(w_value),
    )
    block, left, text_inv = pl.pallas_call(
        project_kernel,
        out_shape=(
            jax.ShapeDtypeStruct((KV_ROWS, 512), BF),
            jax.ShapeDtypeStruct((NSEQ * TEXT, D), BF),
            jax.ShapeDtypeStruct((NSEQ * TEXT, 128), F32),
        ),
        in_specs=[smem] + [vmem] * 11,
        out_specs=(vmem,) * 3,
        scratch_shapes=[pltpu.VMEM((PDIM, 512), F32)],
        compiler_params=pltpu.CompilerParams(vmem_limit_bytes=32 * 2**20),
        name="project",
    )(group, *firsts, *seconds, gain, wk, wv)
    qt = pl.pallas_call(
        query_kernel,
        out_shape=jax.ShapeDtypeStruct((NSEQ * TEXT, 256), BF),
        in_specs=[vmem] * 3,
        out_specs=vmem,
        compiler_params=pltpu.CompilerParams(vmem_limit_bytes=32 * 2**20),
        name="query",
    )(left, text_inv, wq)
    hops = [block] + [
        lax.ppermute(block, "seq", [(i, (i + 2 * k) % seats) for i in range(seats)])
        for k in range(1, seats // 2)
    ]
    other = [lax.ppermute(hop, "seq", [(i, i ^ 1) for i in range(seats)]) for hop in hops]
    attended, z = attend(image_seq, image_start, seat, hops, other, qt, mt, out_grad)
    parts = lax.all_to_all(z.reshape(groups * seats, 8, 128), ("dp", "seq"), 0, 0)
    grad = pl.pallas_call(
        finish_kernel,
        out_shape=jax.ShapeDtypeStruct((PDIM, PDIM), F32),
        in_specs=[vmem] * 4,
        out_specs=vmem,
        compiler_params=pltpu.CompilerParams(vmem_limit_bytes=32 * 2**20),
        name="finish",
    )(parts, lat, inv, u)
    return (attended, grad.reshape(latents.shape))


def solution(mesh):
    in_specs = (
        P(None, "seq", "dp"),
        P("dp", "seq", None),
        P(),
        P(),
        P(),
        P(),
        P(None, "dp"),
        P(None, "dp"),
        P(None, "dp"),
        P(None, "seq", "dp"),
    )
    out_specs = (P(None, "seq", "dp"), P("dp", "seq", None))
    return jax.shard_map(
        on_device, mesh=mesh, in_specs=in_specs, out_specs=out_specs, check_vma=False
    )
```
